256 devices in a mesh: expert: 64 (over z, x, core), mp: 4 (over y).
Axes of the slice: x: 4, y: 4, z: 8, core: 2. Of those that a mesh axis runs over, the one named last changes fastest.
Arguments:
- tokens: bfloat16 [32768, 4096], P('expert', 'mp'), may hold values from -400 to 400
- norm_gain: bfloat16 [4096], P('mp'), may hold values from 0.099609375 to 1.8984375
- router: bfloat16 [4096, 16], replicated, may hold values from -0.09375 to 0.09375
- w_gate: bfloat16 [64, 4096, 1536], P('expert', None, 'mp'), may hold values from -0.09375 to 0.09375
- w_up: bfloat16 [64, 4096, 1536], P('expert', None, 'mp'), may hold values from -0.09375 to 0.09375
- w_down: bfloat16 [64, 1536, 4096], P('expert', 'mp'), may hold values from -0.078125 to 0.078125
- picked: int32 [16, 512], replicated, may hold values from 0 to 32767, as said below
Outputs:
- moe_out: bfloat16 [32768, 4096], P('expert', 'mp')
The draws below stay inside these ranges and needn't reach their ends.
Inputs may be any that keep to these rules, and one draw needn't show every extreme that they name: `picked`: each row names 512 distinct tokens; at most 16 of them lie among the 512 tokens of one index of expert, and for every expert exactly 16 lie among some one device's tokens.
All inputs are finite; a program needn't handle non-finite values.
Results may differ from the reference program's by a relative error of at most 0.0071.
Values may be sent and summed in bfloat16 or wider, within the bound.
A program may use at most 128 MiB of HBM per device.

```python
import jax
import jax.numpy as jnp
from jax import lax

D = 4096
FF = 6144
SLICES = 4
TOK_DEV = 512
CAP = 16
EXPERTS = 16
CAPACITY = 512
TOKENS = 32768


def draw_tokens(key, part):
    key = jax.random.fold_in(key, 2)
    key_row, key_col, key_val = jax.random.split(key, 3)
    column_pos = jnp.arange(D, dtype=jnp.float32) / D
    base = jnp.clip(jax.random.normal(key_val, (TOKENS, D), jnp.float32), -4.0, 4.0)
    col_scale = jnp.exp(jnp.log(3.0) * column_pos + jax.random.uniform(key_col, (D,), jnp.float32, 0.0, jnp.log(3.0)))
    row_scale = jnp.exp(jax.random.uniform(key_row, (TOKENS, 1), jnp.float32, 0.0, jnp.log(10.0)))
    return jnp.clip(base * col_scale[None, :] * row_scale, -400.0, 400.0).astype(jnp.bfloat16)


def draw_picked(key, part):
    key = jax.random.fold_in(key, 1)
    owners = TOKENS // TOK_DEV

    def one_expert(sub_key):
        key_hot, key_local, key_cand, key_order = jax.random.split(sub_key, 4)
        hot_owner = jax.random.randint(key_hot, (), 0, owners)
        local_perm = jax.random.permutation(key_local, TOK_DEV)
        hot_tokens = hot_owner * TOK_DEV + local_perm[:CAP]
        cand_idx = jax.random.permutation(key_cand, (owners - 1) * CAP)[:CAPACITY - CAP]
        other_owner = cand_idx // CAP
        other_owner = other_owner + (other_owner >= hot_owner).astype(other_owner.dtype)
        other_tokens = other_owner * TOK_DEV + local_perm[cand_idx % CAP]
        joined = jnp.concatenate([hot_tokens, other_tokens])
        order = jax.random.permutation(key_order, CAPACITY)
        return joined[order]
    return jax.vmap(one_expert)(jax.random.split(key, EXPERTS)).astype(jnp.int32)


def block_scale(key, dims, shards, low, largest):
    gain, own = 1.0, jax.random.fold_in(key, 6)
    for position, blocks in shards:
        steps = jnp.exp(jax.random.uniform(jax.random.fold_in(own, position), (blocks,), jnp.float32, low / len(shards), largest / len(shards)))
        gain = gain * jnp.repeat(steps, dims[position] // blocks).reshape([-1 if axis == position else 1 for axis in range(len(dims))])
    return gain


def centred(rng, extent, width, reach, cuts=(), kind=jnp.bfloat16):
    entries = width * jax.random.normal(rng, extent, jnp.float32)
    if cuts:
        entries = entries * block_scale(rng, extent, cuts, -0.22, 0.18)
    return jnp.clip(entries, -reach, reach).astype(kind)


def setup_inputs(seed: int = 0) -> dict:
    arg_keys = jax.random.split(jax.random.key(seed), 8)
    tokens = draw_tokens(jax.random.fold_in(arg_keys[7], 71), 0)
    norm_gain = jnp.clip(1.0 + 0.18 * jax.random.normal(arg_keys[1], (D,), jnp.float32), 0.099609375, 1.8984375).astype(jnp.bfloat16)
    router = centred(arg_keys[2], (D, EXPERTS), D ** -0.5, 0.09375)
    w_gate = centred(arg_keys[3], (EXPERTS * SLICES, D, FF // SLICES), D ** -0.5, 0.09375, ((0, 64), (2, 4)))
    w_up = centred(arg_keys[4], (EXPERTS * SLICES, D, FF // SLICES), D ** -0.5, 0.09375, ((0, 64), (2, 4)))
    w_down = centred(arg_keys[5], (EXPERTS * SLICES, FF // SLICES, D), FF ** -0.5, 0.078125, ((0, 64), (1, 4)))
    picked = draw_picked(jax.random.fold_in(arg_keys[7], 71), 0)
    return dict(tokens=tokens, norm_gain=norm_gain, router=router, w_gate=w_gate, w_up=w_up, w_down=w_down, picked=picked)


epsilon = 1e-06

def expert_in(w_stack, expert_id):
    parts = lax.dynamic_slice_in_dim(w_stack, expert_id * SLICES, SLICES, 0)
    return jnp.transpose(parts, (1, 0, 2)).reshape(D, FF)

def expert_down(w_stack, expert_id):
    parts = lax.dynamic_slice_in_dim(w_stack, expert_id * SLICES, SLICES, 0)
    return parts.reshape(FF, D)

def reference(tokens, norm_gain, router, w_gate, w_up, w_down, picked):
    tok_float = tokens.astype(jnp.float32)
    mean_sq = lax.optimization_barrier(jnp.mean(tok_float * tok_float, axis=-1, keepdims=True))
    normed = (tok_float * lax.rsqrt(mean_sq + epsilon) * norm_gain.astype(jnp.float32)).astype(jnp.bfloat16)

    def one_expert(totals, expert_id):
        chosen = lax.dynamic_index_in_dim(picked, expert_id, 0, keepdims=False)
        picked_rows = jnp.take(normed, chosen, axis=0)
        router_col = lax.dynamic_index_in_dim(router, expert_id, 1, keepdims=False)
        logit = jnp.dot(picked_rows, router_col, preferred_element_type=jnp.float32)
        gate_vals = jax.nn.sigmoid(logit).astype(jnp.bfloat16)
        hid_gate = jnp.dot(picked_rows, expert_in(w_gate, expert_id), preferred_element_type=jnp.float32)
        hid_up = jnp.dot(picked_rows, expert_in(w_up, expert_id), preferred_element_type=jnp.float32)
        hidden = (jax.nn.gelu(hid_gate, approximate=True) * hid_up).astype(jnp.bfloat16)
        expert_out = jnp.dot(hidden, expert_down(w_down, expert_id), preferred_element_type=jnp.float32)
        expert_out = expert_out * gate_vals.astype(jnp.float32)[:, None]
        return (totals.at[chosen].add(expert_out), None)
    totals, _ = lax.scan(one_expert, jnp.zeros((TOKENS, D), jnp.float32), jnp.arange(EXPERTS, dtype=jnp.int32))
    return totals.astype(jnp.bfloat16)
```

```python
import functools

import jax
import jax.numpy as jnp
from jax import lax
from jax.experimental import pallas as pl
from jax.experimental.pallas import tpu as pltpu
from jax.sharding import PartitionSpec as P

SLICES = 4
CAP = 16
EPS = 1e-06
MESH = pl.DeviceIdType.MESH
F32 = jnp.float32
BF16 = jnp.bfloat16


def remote(src, dst, send, recv, device):
    return pltpu.make_async_remote_copy(
        src_ref=src,
        dst_ref=dst,
        send_sem=send,
        recv_sem=recv,
        device_id=device,
        device_id_type=MESH,
    )


def rows_contract(lhs, rhs):
    return lax.dot_general(lhs, rhs, (((0,), (0,)), ((), ())), preferred_element_type=F32)


def kernel(
    owners,
    tokens_ref,
    gain_ref,
    router_ref,
    wg_ref,
    wu_ref,
    wd_ref,
    picked_ref,
    out_ref,
    w_cat,
    w_down,
    ssq,
    normed,
    ranked,
    ranked_in,
    take,
    place_t,
    out_buf,
    in_buf,
    rows,
    acc,
    hidden,
    gate,
    core_out,
    core_in,
    own_part,
    y_out,
    y_in,
    x_out,
    x_in,
    ret_out,
    ret_in,
    w_sem,
    ssq_send,
    ssq_recv,
    disp_sem,
    ag_send,
    ag_recv,
    core_send,
    core_recv,
    y_send,
    y_recv,
    x_sem,
    ret_sem,
):
    tok_dev, quarter = tokens_ref.shape
    experts_n, capacity = picked_ref.shape
    sub = quarter // SLICES
    hid = wg_ref.shape[2]
    me = lax.axis_index("expert")
    y = lax.axis_index("mp")
    core = lax.rem(me, 2)
    pair = lax.rem(me // 2, 2)
    my_slice = lax.rem(me, SLICES)
    my_expert = me // SLICES
    sib = (me + 1 - 2 * core, y)
    xpart = (me + 2 - 4 * pair, y)
    y_up = lax.rem(y + 1, 4)
    y_down = lax.rem(y + 3, 4)
    y_far = lax.rem(y + 2, 4)
    up, down = (me, y_up), (me, y_down)

    def peer(r):
        return (lax.rem(me + r, owners), y)

    w_copies = [
        pltpu.make_async_copy(wg_ref.at[0], w_cat.at[:, pl.ds(0, hid)], w_sem.at[0]),
        pltpu.make_async_copy(wu_ref.at[0], w_cat.at[:, pl.ds(hid, hid)], w_sem.at[1]),
        pltpu.make_async_copy(wd_ref.at[0], w_down, w_sem.at[2]),
    ]
    for copy in w_copies:
        copy.start()

    barrier = pltpu.get_barrier_semaphore()

    def greet(r, carry):
        pl.semaphore_signal(barrier, inc=1, device_id=peer(r), device_id_type=MESH)
        return carry

    lax.fori_loop(1, owners, greet, 0)
    for r in range(1, 4):
        pl.semaphore_signal(
            barrier, inc=1, device_id=(me, lax.rem(y + r, 4)), device_id_type=MESH
        )

    lanes = 128
    part = jnp.zeros((tok_dev, lanes), F32)
    for j in range(quarter // lanes):
        piece = tokens_ref[:, j * lanes : (j + 1) * lanes].astype(F32)
        part = part + piece * piece
    ssq[0] = jnp.broadcast_to(jnp.sum(part.T, axis=0, keepdims=True), (8, tok_dev))

    pl.semaphore_wait(barrier, owners - 1 + 3)

    ssq_copies = [
        remote(
            ssq.at[0],
            ssq.at[r],
            ssq_send.at[r - 1],
            ssq_recv.at[r - 1],
            (me, lax.rem(y + r, 4)),
        )
        for r in range(1, 4)
    ]
    for copy in ssq_copies:
        copy.start()

    tri = (
        lax.broadcasted_iota(jnp.int32, (capacity, capacity), 0)
        <= lax.broadcasted_iota(jnp.int32, (capacity, capacity), 1)
    ).astype(F32).astype(BF16)
    rel = picked_ref[...] - me * tok_dev
    mine = (rel >= 0) & (rel < tok_dev)
    mine_f = jnp.where(mine, 1.0, 0.0)
    count = jnp.dot(mine_f.astype(BF16), tri, preferred_element_type=F32)
    ranked[0] = count * mine_f
    ranked[1] = rel.astype(F32)
    slot_no = lax.broadcasted_iota(jnp.int32, (CAP, capacity), 0).astype(F32) + 1.0
    lane_no = lax.broadcasted_iota(jnp.int32, (CAP, tok_dev), 1).astype(F32)
    for e in range(experts_n):
        hit = ranked[0, e : e + 1, :] == slot_no
        chosen = jnp.where(hit, ranked[1, e : e + 1, :] + 1.0, 0.0)
        token = jnp.sum(chosen, axis=1, keepdims=True) - 1.0
        take[e * CAP : (e + 1) * CAP, :] = jnp.where(token == lane_no, 1.0, 0.0).astype(BF16)

    row = picked_ref[pl.ds(my_expert, 1), :]
    low = lax.broadcasted_iota(jnp.int32, (owners, capacity), 0) * tok_dev
    held = jnp.where((row >= low) & (row < low + tok_dev), 1.0, 0.0)
    count_in = jnp.dot(held.astype(BF16), tri, preferred_element_type=F32)
    ranked_in[...] = count_in * held

    def place_owner(i, carry):
        at = pl.multiple_of(i * CAP, CAP)
        hit = ranked_in[pl.ds(i, 1), :] == slot_no
        place_t[pl.ds(at, CAP), :] = jnp.where(hit, 1.0, 0.0).astype(BF16)
        return carry

    lax.fori_loop(0, owners, place_owner, 0)

    for copy in ssq_copies:
        copy.wait_recv()
    total = ssq[0] + ssq[1] + ssq[2] + ssq[3]
    inv = lax.rsqrt(total * (1.0 / (4 * quarter)) + EPS)
    inv = jnp.broadcast_to(inv[0:1, :], (lanes, tok_dev)).T
    for j in range(quarter // lanes):
        cols = slice(j * lanes, (j + 1) * lanes)
        normed[:, cols] = (
            tokens_ref[:, cols].astype(F32) * inv * gain_ref[:, cols].astype(F32)
        ).astype(BF16)

    for s in range(SLICES):
        part_rows = jnp.dot(
            take[...], normed[:, s * sub : (s + 1) * sub], preferred_element_type=F32
        ).astype(BF16)
        for e in range(experts_n):
            out_buf[e * SLICES + s] = part_rows[e * CAP : (e + 1) * CAP, :]

    def dispatch(r, carry):
        d, _ = peer(r)
        remote(
            out_buf.at[d], in_buf.at[me], disp_sem.at[0], disp_sem.at[1], (d, y)
        ).start()
        return carry

    lax.fori_loop(1, owners, dispatch, 0)
    pltpu.make_async_copy(out_buf.at[me], in_buf.at[me], disp_sem.at[1]).start()

    select = jnp.where(
        lax.broadcasted_iota(jnp.int32, (experts_n, lanes), 0) == my_expert, 1.0, 0.0
    ).astype(BF16)
    for j in range(8):
        span = 4 * quarter // 8
        w_cat[j * span : (j + 1) * span, 2 * hid :] = jnp.dot(
            router_ref[j * span : (j + 1) * span, :], select, preferred_element_type=F32
        ).astype(BF16)
    w_copies[0].wait()
    w_copies[1].wait()

    pltpu.make_async_copy(in_buf, in_buf, disp_sem.at[1]).wait()

    def block(at_y, at_pair, at_core):
        return at_y * 4 + at_pair * 2 + at_core

    def ag(b, k, device):
        return remote(rows.at[b], rows.at[b], ag_send.at[k], ag_recv.at[b], device)

    def ag_arrived(b):
        ag(b, 0, sib).wait_recv()

    other = 1 - pair
    own = block(y, pair, core)
    rows[own] = rows_contract(
        place_t[...], in_buf[...].reshape(owners * CAP, sub)
    ).astype(BF16)

    def product(b):
        start = pl.multiple_of(b * sub, sub)
        return jnp.dot(
            rows[b], w_cat[pl.ds(start, sub), :], preferred_element_type=F32
        )

    sends = []

    def go(b, *devices):
        for device in devices:
            copy = ag(b, len(sends), device)
            copy.start()
            sends.append(copy)

    go(own, xpart, up, down, sib)
    acc[...] = product(own)

    def sibling_block(at_y, at_pair):
        b = block(at_y, at_pair, 1 - core)
        ag_arrived(b)
        acc[...] += product(b)

    def own_block(at_y, at_pair, *devices):
        b = block(at_y, at_pair, core)
        ag_arrived(b)
        go(b, *devices, sib)
        acc[...] += product(b)

    own_block(y, other, up, down)
    sibling_block(y, pair)
    own_block(y_down, pair, up)
    own_block(y_up, pair)
    sibling_block(y, other)
    own_block(y_up, other, down)
    own_block(y_down, other)
    sibling_block(y_down, pair)
    sibling_block(y_up, pair)
    sibling_block(y_up, other)
    sibling_block(y_down, other)
    own_block(y_far, pair)
    own_block(y_far, other)
    sibling_block(y_far, pair)
    sibling_block(y_far, other)

    hidden[...] = (
        jax.nn.gelu(acc[:, :hid], approximate=True) * acc[:, hid : 2 * hid]
    ).astype(BF16)
    gate[...] = jax.nn.sigmoid(acc[:, 2 * hid :]).astype(BF16).astype(F32)
    w_copies[2].wait()

    order = [
        (y_far, other),
        (y_far, pair),
        (y_up, other),
        (y_down, other),
        (y_up, pair),
        (y_down, pair),
        (y, other),
        (y, pair),
    ]

    def partial(at_y, at_pair, at_core):
        start = pl.multiple_of(block(at_y, at_pair, at_core) * sub, sub)
        return jnp.dot(
            hidden[...], w_down[:, pl.ds(start, sub)], preferred_element_type=F32
        )

    core_copies = []
    for k, (at_y, at_pair) in enumerate(order):
        core_out[k] = partial(at_y, at_pair, 1 - core).astype(BF16)
        copy = remote(core_out.at[k], core_in.at[k], core_send.at[k], core_recv.at[k], sib)
        copy.start()
        core_copies.append(copy)

    y_copies = []

    def y_go(k, value, device):
        y_out[k] = value.astype(BF16)
        copy = remote(y_out.at[k], y_in.at[k], y_send.at[k], y_recv.at[k], device)
        copy.start()
        y_copies.append(copy)

    def y_arrived(k):
        remote(y_out.at[k], y_in.at[k], y_send.at[k], y_recv.at[k], up).wait_recv()
        return y_in[k].astype(F32)

    def chip_sum(k):
        mine_now = partial(*order[k], core)
        core_copies[k].wait_recv()
        return mine_now + core_in[k].astype(F32)

    y_go(0, chip_sum(0), up)
    y_go(4, chip_sum(1), down)
    own_part[0] = chip_sum(2)
    y_go(3, chip_sum(3), down)
    y_go(2, chip_sum(4), up)
    own_part[1] = chip_sum(5)
    own_part[2] = chip_sum(6)
    own_part[3] = chip_sum(7)
    y_go(1, own_part[0] + y_arrived(0), up)
    y_go(5, own_part[1] + y_arrived(4), down)
    x_out[...] = (own_part[2] + y_arrived(1) + y_arrived(3)).astype(BF16)
    x_copy = remote(x_out, x_in, x_sem.at[0], x_sem.at[1], xpart)
    x_copy.start()
    total_out = own_part[3] + y_arrived(2) + y_arrived(5)
    x_copy.wait_recv()
    total_out = total_out + x_in[...].astype(F32)

    gate_wide = jnp.concatenate([gate[...]] * (sub // lanes), axis=1)
    gated = (total_out * gate_wide).astype(BF16)
    ret_out[...] = (
        jnp.dot(place_t[...], gated, preferred_element_type=F32)
        .astype(BF16)
        .reshape(owners, CAP, sub)
    )
    back = my_slice * experts_n + my_expert

    def give_back(r, carry):
        d, _ = peer(r)
        remote(
            ret_out.at[d], ret_in.at[back], ret_sem.at[0], ret_sem.at[1], (d, y)
        ).start()
        return carry

    lax.fori_loop(1, owners, give_back, 0)
    pltpu.make_async_copy(ret_out.at[me], ret_in.at[back], ret_sem.at[1]).start()

    for copy in ssq_copies + sends + core_copies + y_copies + [x_copy]:
        copy.wait_send()
    most = pl.ds(0, owners - 1)
    pltpu.make_async_copy(out_buf.at[most], out_buf.at[most], disp_sem.at[0]).wait()

    pltpu.make_async_copy(ret_in, ret_in, ret_sem.at[1]).wait()
    for s in range(SLICES):
        arrived = ret_in[s * experts_n : (s + 1) * experts_n].reshape(experts_n * CAP, sub)
        out_ref[:, s * sub : (s + 1) * sub] = rows_contract(take[...], arrived).astype(BF16)
    pltpu.make_async_copy(ret_out.at[most], ret_out.at[most], ret_sem.at[0]).wait()


def per_device(tokens, norm_gain, router, w_gate, w_up, w_down, picked):
    tok_dev, quarter = tokens.shape
    experts_n, capacity = picked.shape
    owners = lax.axis_size("expert")
    sub = quarter // SLICES
    hid = w_gate.shape[2]
    width = 4 * quarter
    dma = pltpu.SemaphoreType.DMA
    vmem = pl.BlockSpec(memory_space=pltpu.VMEM)
    hbm = pl.BlockSpec(memory_space=pl.ANY)
    return pl.pallas_call(
        functools.partial(kernel, owners),
        out_shape=jax.ShapeDtypeStruct((tok_dev, quarter), BF16),
        in_specs=[vmem, vmem, vmem, hbm, hbm, hbm, vmem],
        out_specs=vmem,
        scratch_shapes=[
            pltpu.VMEM((width, 2 * hid + 128), BF16),
            pltpu.VMEM((hid, width), BF16),
            pltpu.VMEM((4, 8, tok_dev), F32),
            pltpu.VMEM((tok_dev, quarter), BF16),
            pltpu.VMEM((2, experts_n, capacity), F32),
            pltpu.VMEM((owners, capacity), F32),
            pltpu.VMEM((experts_n * CAP, tok_dev), BF16),
            pltpu.VMEM((owners * CAP, capacity), BF16),
            pltpu.VMEM((owners, CAP, sub), BF16),
            pltpu.VMEM((owners, CAP, sub), BF16),
            pltpu.VMEM((16, capacity, sub), BF16),
            pltpu.VMEM((capacity, 2 * hid + 128), F32),
            pltpu.VMEM((capacity, hid), BF16),
            pltpu.VMEM((capacity, 128), F32),
            pltpu.VMEM((8, capacity, sub), BF16),
            pltpu.VMEM((8, capacity, sub), BF16),
            pltpu.VMEM((4, capacity, sub), F32),
            pltpu.VMEM((6, capacity, sub), BF16),
            pltpu.VMEM((6, capacity, sub), BF16),
            pltpu.VMEM((capacity, sub), BF16),
            pltpu.VMEM((capacity, sub), BF16),
            pltpu.VMEM((owners, CAP, sub), BF16),
            pltpu.VMEM((owners, CAP, sub), BF16),
            dma((3,)),
            dma((3,)),
            dma((3,)),
            dma((2,)),
            dma((15,)),
            dma((16,)),
            dma((8,)),
            dma((8,)),
            dma((6,)),
            dma((6,)),
            dma((2,)),
            dma((2,)),
        ],
        compiler_params=pltpu.CompilerParams(
            collective_id=0, has_side_effects=True, vmem_limit_bytes=56 * 1024 * 1024
        ),
        cost_estimate=pl.CostEstimate(
            flops=2 * capacity * width * 3 * hid,
            bytes_accessed=3 * 2 * width * hid + 4 * tok_dev * quarter,
            transcendentals=capacity * hid,
        ),
    )(tokens, norm_gain.reshape(1, quarter), router, w_gate, w_up, w_down, picked)


def solution(mesh):
    return jax.shard_map(
        per_device,
        mesh=mesh,
        in_specs=(
            P("expert", "mp"),
            P("mp"),
            P(),
            P("expert", None, "mp"),
            P("expert", None, "mp"),
            P("expert", "mp", None),
            P(),
        ),
        out_specs=P("expert", "mp"),
        check_vma=False,
    )
```

```python
import functools

import jax
import jax.numpy as jnp
from jax import lax
from jax.experimental import pallas as pl
from jax.experimental.pallas import tpu as pltpu
from jax.sharding import PartitionSpec as P

SLICES = 4
CAP = 16
PARTS = 2
LANES = 128
EPS = 1e-06
MESH = pl.DeviceIdType.MESH
F32 = jnp.float32
BF16 = jnp.bfloat16


def remote(src, dst, send, recv, device):
    return pltpu.make_async_remote_copy(
        src_ref=src,
        dst_ref=dst,
        send_sem=send,
        recv_sem=recv,
        device_id=device,
        device_id_type=MESH,
    )


def dot(lhs, rhs):
    return jnp.dot(lhs, rhs, preferred_element_type=F32)


def one_hot(condition):
    return jnp.where(condition, 1.0, 0.0).astype(BF16)


def iota(shape, dim):
    return lax.broadcasted_iota(jnp.int32, shape, dim).astype(F32)


def kernel(
    owners,
    tokens_ref,
    gain_ref,
    router_ref,
    wg_ref,
    wu_ref,
    wd_ref,
    picked_ref,
    out_ref,
    w_cat,
    w_down,
    gains,
    gains_f,
    ranked,
    chosen_tok,
    take,
    take_t,
    place,
    place_t,
    out_buf,
    in_buf,
    rows,
    acc,
    squares,
    hidden,
    gate,
    core_out,
    core_in,
    keep,
    y_out,
    y_in,
    x_out,
    x_in,
    ret_out,
    ret_in,
    w_sem,
    gain_send,
    gain_recv,
    disp_send,
    disp_recv,
    ag_send,
    ag_recv,
    core_send,
    core_recv,
    y_send,
    y_recv,
    x_send,
    x_recv,
    ret_send,
    ret_recv,
):
    tok_dev, quarter = tokens_ref.shape
    experts_n, capacity = picked_ref.shape
    hid = wg_ref.shape[2]
    width = 4 * quarter
    half = capacity // 2
    both = 2 * LANES
    me = lax.axis_index("expert")
    y = lax.axis_index("mp")
    core = lax.rem(me, 2)
    pair = lax.rem(me // 2, 2)
    other = 1 - pair
    my_slice = lax.rem(me, SLICES)
    my_expert = me // SLICES
    sib = (me + 1 - 2 * core, y)
    xpart = (me + 2 - 4 * pair, y)
    y_up = lax.rem(y + 1, 4)
    y_down = lax.rem(y + 3, 4)
    y_far = lax.rem(y + 2, 4)
    up, down = (me, y_up), (me, y_down)

    def peer(r):
        return (lax.rem(me + r, owners), y)

    w_copies = [
        pltpu.make_async_copy(wg_ref.at[0], w_cat.at[:, pl.ds(0, hid)], w_sem.at[0]),
        pltpu.make_async_copy(wu_ref.at[0], w_cat.at[:, pl.ds(hid, hid)], w_sem.at[1]),
        pltpu.make_async_copy(wd_ref.at[0], w_down, w_sem.at[2]),
    ]
    for copy in w_copies:
        copy.start()

    barrier = pltpu.get_barrier_semaphore()

    def greet(r, carry):
        pl.semaphore_signal(barrier, inc=1, device_id=peer(r), device_id_type=MESH)
        return carry

    for r in range(1, 4):
        pl.semaphore_signal(
            barrier, inc=1, device_id=(me, lax.rem(y + r, 4)), device_id_type=MESH
        )
    lax.fori_loop(1, owners, greet, 0)

    tri = one_hot(iota((capacity, capacity), 0) <= iota((capacity, capacity), 1))
    rel = picked_ref[...] - me * tok_dev
    mine = jnp.where((rel >= 0) & (rel < tok_dev), 1.0, 0.0)
    ranked[0] = dot(mine.astype(BF16), tri) * mine
    ranked[1] = rel.astype(F32) + 1.0
    slot_no = iota((CAP, capacity), 0) + 1.0
    lane_no = iota((CAP, tok_dev), 1)
    for e in range(experts_n):
        hit = ranked[0, e : e + 1, :] == slot_no
        found = jnp.where(hit, ranked[1, e : e + 1, :], 0.0)
        token = jnp.sum(found, axis=1, keepdims=True) - 1.0
        take[e * CAP : (e + 1) * CAP, :] = one_hot(token == lane_no)
        chosen_tok[e * CAP : (e + 1) * CAP, :] = jnp.broadcast_to(token, (CAP, LANES))

    def gather(part):
        for p in range(2):
            start = p * quarter // 2 + part * both
            found = dot(take[...], tokens_ref[:, start : start + both]).astype(BF16)
            for e in range(experts_n):
                for c in range(2):
                    out_buf[part, e * SLICES + p * 2 + c] = found[
                        e * CAP : (e + 1) * CAP, c * LANES : (c + 1) * LANES
                    ]

    gather(0)
    gains[y] = jnp.concatenate([gain_ref[...], gain_ref[...]], axis=0)

    pl.semaphore_wait(barrier, owners - 1 + 3)

    def dispatch(part):
        def start(r, carry):
            d, _ = peer(r)
            remote(
                out_buf.at[part, d],
                in_buf.at[part, me],
                disp_send.at[part],
                disp_recv.at[part],
                (d, y),
            ).start()
            return carry

        lax.fori_loop(1, owners, start, 0)
        pltpu.make_async_copy(
            out_buf.at[part, me], in_buf.at[part, me], disp_recv.at[part]
        ).start()

    gain_copies = []
    for r in range(1, 4):
        copy = remote(
            gains.at[y],
            gains.at[y],
            gain_send.at[r - 1],
            gain_recv.at[y],
            (me, lax.rem(y + r, 4)),
        )
        copy.start()
        gain_copies.append(copy)
    dispatch(0)
    gather(1)
    dispatch(1)

    row = picked_ref[pl.ds(my_expert, 1), :]
    low = lax.broadcasted_iota(jnp.int32, (owners, capacity), 0) * tok_dev
    held = jnp.where((row >= low) & (row < low + tok_dev), 1.0, 0.0)
    slot_at = dot(held.astype(BF16), tri) - 1.0 + iota((owners, capacity), 0) * CAP
    flat = jnp.sum(held * slot_at, axis=0, keepdims=True)
    flat_col = jnp.broadcast_to(flat, (LANES, capacity)).T
    down_no = iota((LANES, capacity), 0)
    across_no = iota((capacity, LANES), 1)
    for j in range(owners * CAP // LANES):
        span = slice(j * LANES, (j + 1) * LANES)
        place_t[span, :] = one_hot(flat == down_no + j * LANES)
        place[:, span] = one_hot(flat_col == across_no + j * LANES)
    take_t[...] = one_hot(chosen_tok[...].T[0:1, :] == iota((tok_dev, experts_n * CAP), 0))

    select = one_hot(iota((experts_n, LANES), 0) == my_expert.astype(F32))
    for r in range(1, 4):
        at = lax.rem(y + r, 4)
        remote(gains.at[at], gains.at[at], gain_send.at[0], gain_recv.at[at], up).wait_recv()
    for at in range(4):
        gains_f[at * 8 : (at + 1) * 8, :] = gains[at][:8, :].astype(F32)
    w_copies[0].wait()
    w_copies[1].wait()

    def scale(q, carry):
        start = pl.multiple_of(q * LANES, LANES)
        column = jnp.broadcast_to(gains_f[pl.ds(q, 1), :], (LANES, LANES)).T
        for j in range(2 * hid // LANES):
            cols = slice(j * LANES, (j + 1) * LANES)
            w_cat[pl.ds(start, LANES), cols] = (
                w_cat[pl.ds(start, LANES), cols].astype(F32) * column
            ).astype(BF16)
        routed = lax.dot_general(
            router_ref[:, pl.ds(start, LANES)],
            select,
            (((0,), (0,)), ((), ())),
            preferred_element_type=F32,
        )
        w_cat[pl.ds(start, LANES), 2 * hid :] = (routed * column).astype(BF16)
        return carry

    lax.fori_loop(0, width // LANES, scale, 0)

    def block(at_y, at_pair):
        return at_y * 2 + at_pair

    def ag(part, b, c, h, k, device):
        at = rows.at[part, b, c, pl.ds(h * half, half)]
        number = ((part * 8 + b) * 2 + c) * 2 + h
        return remote(at, at, ag_send.at[k], ag_recv.at[number], device)

    sends = []

    def go(part, b, h, *devices):
        for device in devices:
            copy = ag(part, b, core, h, len(sends), device)
            copy.start()
            sends.append(copy)

    def pass_on(part, b, h, *devices):
        ag(part, b, core, h, 0, sib).wait_recv()
        go(part, b, h, *devices, sib)

    def begin(part):
        pltpu.make_async_copy(in_buf.at[part], in_buf.at[part], disp_recv.at[part]).wait()
        b = block(y, pair)
        rows[part, b, core] = dot(
            place[...], in_buf[part].reshape(owners * CAP, LANES)
        ).astype(BF16)
        for h in range(2):
            go(part, b, h, xpart, up, down, sib)

    def from_neighbours(part):
        pass_on(part, block(y_down, pair), 0, up)
        pass_on(part, block(y_up, pair), 1, down)
        pass_on(part, block(y_down, pair), 1)
        pass_on(part, block(y_up, pair), 0)

    def from_partner(part):
        for h in range(2):
            pass_on(part, block(y, other), h, up, down)

    def from_far(part):
        for h in range(2):
            pass_on(part, block(y_far, pair), h, xpart)

    def from_corners(part):
        for h in range(2):
            pass_on(part, block(y_down, other), h)
            pass_on(part, block(y_up, other), h)

    def from_far_corner(part):
        for h in range(2):
            pass_on(part, block(y_far, other), h)

    def product(part, at_y, at_pair, first=False):
        b = block(at_y, at_pair)
        for h in range(2):
            ag(part, b, 1 - core, h, 0, sib).wait_recv()
        start = pl.multiple_of(
            at_y * quarter + at_pair * (quarter // 2) + part * both, both
        )
        left, right = rows[part, b, 0], rows[part, b, 1]
        new = dot(jnp.concatenate([left, right], axis=1), w_cat[pl.ds(start, both), :])
        left, right = left.astype(F32), right.astype(F32)
        square = left * left + right * right
        if first:
            acc[...] = new
            squares[...] = square
        else:
            acc[...] += new
            squares[...] += square

    begin(0)
    from_neighbours(0)
    begin(1)
    from_partner(0)
    product(0, y, pair, first=True)
    product(0, y_down, pair)
    product(0, y_up, pair)
    product(0, y, other)
    from_far(0)
    from_neighbours(1)
    from_partner(1)
    from_corners(0)
    product(1, y, pair)
    product(0, y_far, pair)
    product(1, y_down, pair)
    product(1, y_up, pair)
    product(1, y, other)
    from_far(1)
    from_far_corner(0)
    product(0, y_down, other)
    product(0, y_up, other)
    product(0, y_far, other)
    from_corners(1)
    from_far_corner(1)
    product(1, y_far, pair)
    product(1, y_down, other)
    product(1, y_up, other)
    product(1, y_far, other)

    total = jnp.sum(squares[...], axis=1, keepdims=True)
    inv = lax.rsqrt(total * (1.0 / width) + EPS)
    hidden[...] = (
        jax.nn.gelu(acc[:, :hid] * inv, approximate=True) * (acc[:, hid : 2 * hid] * inv)
    ).astype(BF16)
    gate[...] = jax.nn.sigmoid(acc[:, 2 * hid :] * inv).astype(BF16).astype(F32)
    w_copies[2].wait()

    targets = [
        (y_far, other),
        (y_up, other),
        (y_down, other),
        (y_far, pair),
        (y_up, pair),
        (y_down, pair),
        (y, other),
        (y, pair),
    ]
    top, bottom = slice(0, half), slice(half, capacity)
    core_copies = {}

    def partials(part):
        for k, (at_y, at_pair) in enumerate(targets):
            start = pl.multiple_of(
                at_y * quarter + at_pair * (quarter // 2) + part * both, both
            )
            both_cores = dot(hidden[...], w_down[:, pl.ds(start, both)])
            low_half, high_half = both_cores[:, :LANES], both_cores[:, LANES:]
            keep[part, k] = jnp.where(core == 0, low_half, high_half)
            core_out[part, k] = jnp.where(core == 0, high_half, low_half).astype(BF16)
            number = part * 8 + k
            copy = remote(
                core_out.at[part, k],
                core_in.at[part, k],
                core_send.at[number],
                core_recv.at[number],
                sib,
            )
            copy.start()
            core_copies[part, k] = copy

    def chip(part, k):
        core_copies[part, k].wait_recv()
        return keep[part, k] + core_in[part, k].astype(F32)

    moved = []

    def y_copy(part, way, m):
        number = (part * 2 + way) * 5 + m
        return remote(
            y_out.at[part, way, m],
            y_in.at[part, way, m],
            y_send.at[number],
            y_recv.at[number],
            (up, down)[way],
        )

    def y_go(part, way, m, value):
        y_out[part, way, m] = value.astype(BF16)
        copy = y_copy(part, way, m)
        copy.start()
        moved.append(copy)

    def y_got(part, way, m):
        y_copy(part, way, m).wait_recv()
        return y_in[part, way, m].astype(F32)

    def x_copy(part, m):
        number = part * 4 + m
        return remote(
            x_out.at[part, m], x_in.at[part, m], x_send.at[number], x_recv.at[number], xpart
        )

    def x_go(part, m, value):
        x_out[part, m] = value.astype(BF16)
        copy = x_copy(part, m)
        copy.start()
        moved.append(copy)

    def x_got(part, m):
        x_copy(part, m).wait_recv()
        return x_in[part, m].astype(F32)

    def send_other(part):
        value = chip(part, 0)
        x_go(part, 0, value[top])
        x_go(part, 1, value[bottom])
        for way in range(2):
            value = chip(part, 1 + way)
            y_go(part, way, 0, value[top])
            y_go(part, way, 1, value[bottom])

    def send_direct(part):
        value = chip(part, 4)
        y_go(part, 0, 2, value[top])
        keep[part, 4, bottom] = value[bottom]
        value = chip(part, 5)
        y_go(part, 1, 2, value[bottom])
        keep[part, 5, top] = value[top]

    def send_far(part):
        value = chip(part, 3)
        y_go(part, 1, 3, value[top] + x_got(part, 0))
        y_go(part, 0, 3, value[bottom] + x_got(part, 1))

    def send_merged(part):
        y_go(part, 1, 4, keep[part, 5, top] + y_got(part, 1, 3))
        y_go(part, 0, 4, keep[part, 4, bottom] + y_got(part, 0, 3))

    def send_partner(part):
        value = chip(part, 6)
        x_go(part, 2, value[top] + y_got(part, 0, 0) + y_got(part, 1, 0))
        x_go(part, 3, value[bottom] + y_got(part, 0, 1) + y_got(part, 1, 1))

    back = my_slice * experts_n + my_expert

    def give_back(part):
        value = chip(part, 7)
        upper = value[top] + y_got(part, 0, 2) + y_got(part, 1, 4) + x_got(part, 2)
        lower = value[bottom] + y_got(part, 1, 2) + y_got(part, 0, 4) + x_got(part, 3)
        gated = (jnp.concatenate([upper, lower], axis=0) * gate[...]).astype(BF16)
        ret_out[part] = dot(place_t[...], gated).astype(BF16).reshape(owners, CAP, LANES)

        def start(r, carry):
            d, _ = peer(r)
            remote(
                ret_out.at[part, d],
                ret_in.at[part, back],
                ret_send.at[part],
                ret_recv.at[part],
                (d, y),
            ).start()
            return carry

        lax.fori_loop(1, owners, start, 0)
        pltpu.make_async_copy(
            ret_out.at[part, me], ret_in.at[part, back], ret_recv.at[part]
        ).start()

    partials(0)
    send_other(0)
    send_direct(0)
    partials(1)
    send_far(0)
    send_other(1)
    send_partner(0)
    send_merged(0)
    send_far(1)
    send_direct(1)
    send_partner(1)
    send_merged(1)
    give_back(0)
    give_back(1)

    most = pl.ds(0, owners - 1)
    for copy in gain_copies + sends + list(core_copies.values()) + moved:
        copy.wait_send()
    for part in range(PARTS):
        sent = out_buf.at[part, most]
        pltpu.make_async_copy(sent, sent, disp_send.at[part]).wait()

    for part in range(PARTS):
        pltpu.make_async_copy(ret_in.at[part], ret_in.at[part], ret_recv.at[part]).wait()
        for p in range(2):
            sides = [
                ret_in[part, (p * 2 + c) * experts_n : (p * 2 + c + 1) * experts_n].reshape(
                    experts_n * CAP, LANES
                )
                for c in range(2)
            ]
            start = p * quarter // 2 + part * both
            out_ref[:, start : start + both] = dot(
                take_t[...], jnp.concatenate(sides, axis=1)
            ).astype(BF16)
    for part in range(PARTS):
        sent = ret_out.at[part, most]
        pltpu.make_async_copy(sent, sent, ret_send.at[part]).wait()


def per_device(tokens, norm_gain, router, w_gate, w_up, w_down, picked):
    tok_dev, quarter = tokens.shape
    experts_n, capacity = picked.shape
    owners = lax.axis_size("expert")
    hid = w_gate.shape[2]
    width = 4 * quarter
    half = capacity // 2
    slots = experts_n * CAP
    dma = pltpu.SemaphoreType.DMA
    vmem = pl.BlockSpec(memory_space=pltpu.VMEM)
    hbm = pl.BlockSpec(memory_space=pl.ANY)
    return pl.pallas_call(
        functools.partial(kernel, owners),
        out_shape=jax.ShapeDtypeStruct((tok_dev, quarter), BF16),
        in_specs=[vmem, vmem, vmem, hbm, hbm, hbm, vmem],
        out_specs=vmem,
        scratch_shapes=[
            pltpu.VMEM((width, 2 * hid + LANES), BF16),
            pltpu.VMEM((hid, width), BF16),
            pltpu.VMEM((4, 16, LANES), BF16),
            pltpu.VMEM((32, LANES), F32),
            pltpu.VMEM((2, experts_n, capacity), F32),
            pltpu.VMEM((slots, LANES), F32),
            pltpu.VMEM((slots, tok_dev), BF16),
            pltpu.VMEM((tok_dev, slots), BF16),
            pltpu.VMEM((capacity, owners * CAP), BF16),
            pltpu.VMEM((owners * CAP, capacity), BF16),
            pltpu.VMEM((PARTS, owners, CAP, LANES), BF16),
            pltpu.VMEM((PARTS, owners, CAP, LANES), BF16),
            pltpu.VMEM((PARTS, 8, 2, capacity, LANES), BF16),
            pltpu.VMEM((capacity, 2 * hid + LANES), F32),
            pltpu.VMEM((capacity, LANES), F32),
            pltpu.VMEM((capacity, hid), BF16),
            pltpu.VMEM((capacity, LANES), F32),
            pltpu.VMEM((PARTS, 8, capacity, LANES), BF16),
            pltpu.VMEM((PARTS, 8, capacity, LANES), BF16),
            pltpu.VMEM((PARTS, 8, capacity, LANES), F32),
            pltpu.VMEM((PARTS, 2, 5, half, LANES), BF16),
            pltpu.VMEM((PARTS, 2, 5, half, LANES), BF16),
            pltpu.VMEM((PARTS, 4, half, LANES), BF16),
            pltpu.VMEM((PARTS, 4, half, LANES), BF16),
            pltpu.VMEM((PARTS, owners, CAP, LANES), BF16),
            pltpu.VMEM((PARTS, owners, CAP, LANES), BF16),
            dma((3,)),
            dma((3,)),
            dma((4,)),
            dma((PARTS,)),
            dma((PARTS,)),
            dma((60,)),
            dma((64,)),
            dma((16,)),
            dma((16,)),
            dma((20,)),
            dma((20,)),
            dma((8,)),
            dma((8,)),
            dma((PARTS,)),
            dma((PARTS,)),
        ],
        compiler_params=pltpu.CompilerParams(
            collective_id=0, has_side_effects=True, vmem_limit_bytes=56 * 1024 * 1024
        ),
        cost_estimate=pl.CostEstimate(
            flops=2 * capacity * width * 3 * hid,
            bytes_accessed=3 * 2 * width * hid + 4 * tok_dev * quarter,
            transcendentals=capacity * hid,
        ),
    )(
        tokens,
        norm_gain.reshape(quarter // LANES, LANES),
        router.T,
        w_gate,
        w_up,
        w_down,
        picked,
    )


def solution(mesh):
    return jax.shard_map(
        per_device,
        mesh=mesh,
        in_specs=(
            P("expert", "mp"),
            P("mp"),
            P(),
            P("expert", None, "mp"),
            P("expert", None, "mp"),
            P("expert", "mp", None),
            P(),
        ),
        out_specs=P("expert", "mp"),
        check_vma=False,
    )
```

```python
import functools

import jax
import jax.numpy as jnp
from jax import lax
from jax.experimental import pallas as pl
from jax.experimental.pallas import tpu as pltpu
from jax.sharding import PartitionSpec as P

SLICES = 4
CAP = 16
PARTS = 2
LANES = 128
EPS = 1e-06
MESH = pl.DeviceIdType.MESH
F32 = jnp.float32
BF16 = jnp.bfloat16


def remote(src, dst, send, recv, device):
    return pltpu.make_async_remote_copy(
        src_ref=src,
        dst_ref=dst,
        send_sem=send,
        recv_sem=recv,
        device_id=device,
        device_id_type=MESH,
    )


def dot(lhs, rhs):
    return jnp.dot(lhs, rhs, preferred_element_type=F32)


def one_hot(condition):
    return jnp.where(condition, 1.0, 0.0).astype(BF16)


def iota(shape, dim):
    return lax.broadcasted_iota(jnp.int32, shape, dim).astype(F32)


def kernel(
    owners,
    tokens_hbm,
    gain_hbm,
    router_hbm,
    wg_ref,
    wu_ref,
    wd_ref,
    picked_hbm,
    out_ref,
    tokens_ref,
    gain_ref,
    router_ref,
    picked_ref,
    w_cat,
    w_down,
    gains,
    gains_f,
    ranked,
    chosen_tok,
    take,
    take_t,
    place,
    place_t,
    out_buf,
    in_buf,
    rows,
    acc,
    squares,
    hidden,
    gate,
    core_out,
    core_in,
    keep,
    y_out,
    y_in,
    x_out,
    x_in,
    ret_out,
    ret_in,
    in_sem,
    w_sem,
    gain_send,
    gain_recv,
    disp_send,
    disp_recv,
    ag_send,
    ag_recv,
    core_send,
    core_recv,
    y_send,
    y_recv,
    x_send,
    x_recv,
    ret_send,
    ret_recv,
):
    tok_dev, quarter = tokens_ref.shape
    experts_n, capacity = picked_ref.shape
    hid = wg_ref.shape[2]
    width = 4 * quarter
    half = capacity // 2
    both = 2 * LANES
    me = lax.axis_index("expert")
    y = lax.axis_index("mp")
    core = lax.rem(me, 2)
    pair = lax.rem(me // 2, 2)
    other = 1 - pair
    my_slice = lax.rem(me, SLICES)
    my_expert = me // SLICES
    sib = (me + 1 - 2 * core, y)
    xpart = (me + 2 - 4 * pair, y)
    y_up = lax.rem(y + 1, 4)
    y_down = lax.rem(y + 3, 4)
    y_far = lax.rem(y + 2, 4)
    up, down = (me, y_up), (me, y_down)

    def peer(r):
        return (lax.rem(me + r, owners), y)

    barrier = pltpu.get_barrier_semaphore()

    def greet(r, carry):
        pl.semaphore_signal(barrier, inc=1, device_id=peer(r), device_id_type=MESH)
        return carry

    for r in range(1, 4):
        pl.semaphore_signal(
            barrier, inc=1, device_id=(me, lax.rem(y + r, 4)), device_id_type=MESH
        )
    lax.fori_loop(1, owners, greet, 0)

    in_copies = [
        pltpu.make_async_copy(src, dst, in_sem.at[k])
        for k, (src, dst) in enumerate(
            [
                (picked_hbm, picked_ref),
                (tokens_hbm, tokens_ref),
                (gain_hbm, gain_ref),
                (router_hbm, router_ref),
            ]
        )
    ]
    w_copies = [
        pltpu.make_async_copy(wg_ref.at[0], w_cat.at[:, pl.ds(0, hid)], w_sem.at[0]),
        pltpu.make_async_copy(wu_ref.at[0], w_cat.at[:, pl.ds(hid, hid)], w_sem.at[1]),
    ]
    for copy in in_copies + w_copies:
        copy.start()

    tri = one_hot(iota((capacity, capacity), 0) <= iota((capacity, capacity), 1))
    in_copies[0].wait()
    rel = picked_ref[...] - me * tok_dev
    mine = jnp.where((rel >= 0) & (rel < tok_dev), 1.0, 0.0)
    ranked[0] = dot(mine.astype(BF16), tri) * mine
    ranked[1] = rel.astype(F32) + 1.0
    slot_no = iota((CAP, capacity), 0) + 1.0
    lane_no = iota((CAP, tok_dev), 1)
    for e in range(experts_n):
        hit = ranked[0, e : e + 1, :] == slot_no
        found = jnp.where(hit, ranked[1, e : e + 1, :], 0.0)
        token = jnp.sum(found, axis=1, keepdims=True) - 1.0
        take[e * CAP : (e + 1) * CAP, :] = one_hot(token == lane_no)
        chosen_tok[e * CAP : (e + 1) * CAP, :] = jnp.broadcast_to(token, (CAP, LANES))

    row = picked_ref[pl.ds(my_expert, 1), :]
    low = lax.broadcasted_iota(jnp.int32, (owners, capacity), 0) * tok_dev
    held = jnp.where((row >= low) & (row < low + tok_dev), 1.0, 0.0)
    slot_at = dot(held.astype(BF16), tri) - 1.0 + iota((owners, capacity), 0) * CAP
    flat = jnp.sum(held * slot_at, axis=0, keepdims=True)
    flat_col = jnp.broadcast_to(flat, (LANES, capacity)).T
    down_no = iota((LANES, capacity), 0)
    across_no = iota((capacity, LANES), 1)
    for j in range(owners * CAP // LANES):
        span = slice(j * LANES, (j + 1) * LANES)
        place_t[span, :] = one_hot(flat == down_no + j * LANES)
        place[:, span] = one_hot(flat_col == across_no + j * LANES)
    take_t[...] = one_hot(chosen_tok[...].T[0:1, :] == iota((tok_dev, experts_n * CAP), 0))

    def gather(part):
        for p in range(2):
            start = p * quarter // 2 + part * both
            found = dot(take[...], tokens_ref[:, start : start + both]).astype(BF16)
            for e in range(experts_n):
                for c in range(2):
                    out_buf[part, e * SLICES + p * 2 + c] = found[
                        e * CAP : (e + 1) * CAP, c * LANES : (c + 1) * LANES
                    ]

    in_copies[1].wait()
    gather(0)
    gather(1)
    in_copies[2].wait()
    in_copies[3].wait()
    select = one_hot(iota((experts_n, LANES), 0) == my_expert.astype(F32))
    for j in range(8):
        span = slice(j * width // 8, (j + 1) * width // 8)
        w_cat[span, 2 * hid :] = lax.dot_general(
            router_ref[:, span],
            select,
            (((0,), (0,)), ((), ())),
            preferred_element_type=F32,
        ).astype(BF16)
    gains[y] = jnp.concatenate([gain_ref[...], gain_ref[...]], axis=0)

    pl.semaphore_wait(barrier, owners - 1 + 3)

    targets = [
        (y_far, other),
        (y_up, other),
        (y_down, other),
        (y_far, pair),
        (y_up, pair),
        (y_down, pair),
        (y, other),
        (y, pair),
    ]

    def load_down():
        for part in range(PARTS):
            for k, (at_y, at_pair) in enumerate(targets):
                for side, c in enumerate((core, 1 - core)):
                    start = at_y * quarter + at_pair * (quarter // 2) + part * both + c * LANES
                    pltpu.make_async_copy(
                        wd_ref.at[0, :, pl.ds(pl.multiple_of(start, LANES), LANES)],
                        w_down.at[side, :, pl.ds((part * 8 + k) * LANES, LANES)],
                        w_sem.at[2],
                    ).start()

    def dispatch(part):
        for side in range(2):

            def start(j, carry):
                d = 2 * lax.rem(me // 2 + j, owners // 2) + side
                remote(
                    out_buf.at[part, d],
                    in_buf.at[part, me],
                    disp_send.at[part],
                    disp_recv.at[part],
                    (d, y),
                ).start()
                return carry

            first = 1 - core if side == 0 else core
            lax.fori_loop(first, owners // 2, start, 0)
        pltpu.make_async_copy(
            out_buf.at[part, me], in_buf.at[part, me], disp_recv.at[part]
        ).start()

    gain_copies = []
    for r in range(1, 4):
        copy = remote(
            gains.at[y],
            gains.at[y],
            gain_send.at[r - 1],
            gain_recv.at[y],
            (me, lax.rem(y + r, 4)),
        )
        copy.start()
        gain_copies.append(copy)
    dispatch(0)
    dispatch(1)
    load_down()

    for r in range(1, 4):
        at = lax.rem(y + r, 4)
        remote(gains.at[at], gains.at[at], gain_send.at[0], gain_recv.at[at], up).wait_recv()
    for at in range(4):
        gains_f[at * 8 : (at + 1) * 8, :] = gains[at][:8, :].astype(F32)
    w_copies[0].wait()
    w_copies[1].wait()

    def scale(q, carry):
        start = pl.multiple_of(q * LANES, LANES)
        column = jnp.broadcast_to(gains_f[pl.ds(q, 1), :], (LANES, LANES)).T
        for j in range(2 * hid // LANES + 1):
            cols = slice(j * LANES, (j + 1) * LANES)
            w_cat[pl.ds(start, LANES), cols] = (
                w_cat[pl.ds(start, LANES), cols].astype(F32) * column
            ).astype(BF16)
        return carry

    lax.fori_loop(0, width // LANES, scale, 0, unroll=4)

    def block(at_y, at_pair):
        return at_y * 2 + at_pair

    def ag(part, b, c, h, k, device):
        at = rows.at[part, b, c, pl.ds(h * half, half)]
        number = ((part * 8 + b) * 2 + c) * 2 + h
        return remote(at, at, ag_send.at[k], ag_recv.at[number], device)

    sends = []

    def go(part, b, h, *devices):
        for device in devices:
            copy = ag(part, b, core, h, len(sends), device)
            copy.start()
            sends.append(copy)

    def pass_on(part, b, h, *devices):
        ag(part, b, core, h, 0, sib).wait_recv()
        go(part, b, h, *devices, sib)

    def begin(part):
        pltpu.make_async_copy(in_buf.at[part], in_buf.at[part], disp_recv.at[part]).wait()
        b = block(y, pair)
        rows[part, b, core] = dot(
            place[...], in_buf[part].reshape(owners * CAP, LANES)
        ).astype(BF16)
        for h in range(2):
            go(part, b, h, xpart, up)
            go(part, b, 1 - h, down)
            go(part, b, h, sib)

    def from_neighbours(part):
        pass_on(part, block(y_down, pair), 0, up)
        pass_on(part, block(y_up, pair), 1, down)

    def rest_of_neighbours(part):
        pass_on(part, block(y_down, pair), 1)
        pass_on(part, block(y_up, pair), 0)

    def from_partner(part, h):
        pass_on(part, block(y, other), h, up, down)

    def from_far(part):
        for h in range(2):
            pass_on(part, block(y_far, pair), h, xpart)

    def from_corners(part):
        for h in range(2):
            pass_on(part, block(y_down, other), h)
            pass_on(part, block(y_up, other), h)

    def from_far_corner(part):
        for h in range(2):
            pass_on(part, block(y_far, other), h)

    def product(part, at_y, at_pair, first=False):
        b = block(at_y, at_pair)
        for h in range(2):
            ag(part, b, 1 - core, h, 0, sib).wait_recv()
        start = pl.multiple_of(
            at_y * quarter + at_pair * (quarter // 2) + part * both, both
        )
        left, right = rows[part, b, 0], rows[part, b, 1]
        new = dot(jnp.concatenate([left, right], axis=1), w_cat[pl.ds(start, both), :])
        left, right = left.astype(F32), right.astype(F32)
        square = left * left + right * right
        if first:
            acc[...] = new
            squares[...] = square
        else:
            acc[...] += new
            squares[...] += square

    begin(0)
    from_neighbours(0)
    from_partner(0, 0)
    begin(1)
    from_partner(0, 1)
    rest_of_neighbours(0)
    product(0, y, pair, first=True)
    product(0, y_down, pair)
    from_far(0)
    product(0, y_up, pair)
    from_neighbours(1)
    from_partner(1, 0)
    from_partner(1, 1)
    rest_of_neighbours(1)
    product(0, y, other)
    product(1, y, pair)
    product(0, y_far, pair)
    from_corners(0)
    product(1, y_down, pair)
    from_far(1)
    product(1, y_up, pair)
    product(1, y, other)
    from_far_corner(0)
    product(0, y_down, other)
    product(0, y_up, other)
    product(0, y_far, other)
    from_corners(1)
    product(1, y_far, pair)
    product(1, y_down, other)
    product(1, y_up, other)
    from_far_corner(1)
    product(1, y_far, other)

    total = jnp.sum(squares[...], axis=1, keepdims=True)
    inv = lax.rsqrt(total * (1.0 / width) + EPS)
    hidden[...] = (
        jax.nn.gelu(acc[:, :hid] * inv, approximate=True) * (acc[:, hid : 2 * hid] * inv)
    ).astype(BF16)
    gate[...] = jax.nn.sigmoid(acc[:, 2 * hid :] * inv).astype(BF16).astype(F32)
    pltpu.make_async_copy(w_down, w_down, w_sem.at[2]).wait()

    top, bottom = slice(0, half), slice(half, capacity)
    core_copies = {}

    def partial(part, k, side):
        start = (part * 8 + k) * LANES
        return dot(hidden[...], w_down[side, :, start : start + both])

    def for_sibling(part, *firsts):
        for first in firsts:
            value = partial(part, first, 1)
            for k in (first, first + 1):
                at = (k - first) * LANES
                core_out[part, k] = value[:, at : at + LANES].astype(BF16)
                number = part * 8 + k
                copy = remote(
                    core_out.at[part, k],
                    core_in.at[part, k],
                    core_send.at[number],
                    core_recv.at[number],
                    sib,
                )
                copy.start()
                core_copies[part, k] = copy

    def for_me(part, *firsts):
        for first in firsts:
            value = partial(part, first, 0)
            keep[part, first] = value[:, :LANES]
            keep[part, first + 1] = value[:, LANES:]

    def chip(part, k):
        core_copies[part, k].wait_recv()
        return keep[part, k] + core_in[part, k].astype(F32)

    moved = []

    def y_copy(part, way, m):
        number = (part * 2 + way) * 5 + m
        return remote(
            y_out.at[part, way, m],
            y_in.at[part, way, m],
            y_send.at[number],
            y_recv.at[number],
            (up, down)[way],
        )

    def y_go(part, way, m, value):
        y_out[part, way, m] = value.astype(BF16)
        copy = y_copy(part, way, m)
        copy.start()
        moved.append(copy)

    def y_got(part, way, m):
        y_copy(part, way, m).wait_recv()
        return y_in[part, way, m].astype(F32)

    def x_copy(part, m):
        number = part * 4 + m
        return remote(
            x_out.at[part, m], x_in.at[part, m], x_send.at[number], x_recv.at[number], xpart
        )

    def x_go(part, m, value):
        x_out[part, m] = value.astype(BF16)
        copy = x_copy(part, m)
        copy.start()
        moved.append(copy)

    def x_got(part, m):
        x_copy(part, m).wait_recv()
        return x_in[part, m].astype(F32)

    def send_corner(part):
        value = chip(part, 0)
        x_go(part, 0, value[top])
        x_go(part, 1, value[bottom])

    def send_other(part):
        for way in range(2):
            value = chip(part, 1 + way)
            y_go(part, way, 0, value[top])
            y_go(part, way, 1, value[bottom])

    def send_direct(part):
        value = chip(part, 4)
        y_go(part, 0, 2, value[top])
        keep[part, 4, bottom] = value[bottom]
        value = chip(part, 5)
        y_go(part, 1, 2, value[bottom])
        keep[part, 5, top] = value[top]

    def send_far(part):
        value = chip(part, 3)
        y_go(part, 1, 3, value[top] + x_got(part, 0))
        y_go(part, 0, 3, value[bottom] + x_got(part, 1))

    def send_merged(part):
        y_go(part, 1, 4, keep[part, 5, top] + y_got(part, 1, 3))
        y_go(part, 0, 4, keep[part, 4, bottom] + y_got(part, 0, 3))

    def send_partner(part):
        value = chip(part, 6)
        x_go(part, 2, value[top] + y_got(part, 0, 0) + y_got(part, 1, 0))
        x_go(part, 3, value[bottom] + y_got(part, 0, 1) + y_got(part, 1, 1))

    back = my_slice * experts_n + my_expert

    def give_back(part):
        value = chip(part, 7)
        upper = value[top] + y_got(part, 0, 2) + y_got(part, 1, 4) + x_got(part, 2)
        lower = value[bottom] + y_got(part, 1, 2) + y_got(part, 0, 4) + x_got(part, 3)
        gated = (jnp.concatenate([upper, lower], axis=0) * gate[...]).astype(BF16)
        ret_out[part] = dot(place_t[...], gated).astype(BF16).reshape(owners, CAP, LANES)

        def start(r, carry):
            d, _ = peer(r)
            remote(
                ret_out.at[part, d],
                ret_in.at[part, back],
                ret_send.at[part],
                ret_recv.at[part],
                (d, y),
            ).start()
            return carry

        lax.fori_loop(1, owners, start, 0)
        pltpu.make_async_copy(
            ret_out.at[part, me], ret_in.at[part, back], ret_recv.at[part]
        ).start()

    for_sibling(0, 0, 2)
    for_me(0, 0)
    send_corner(0)
    for_me(0, 2)
    send_other(0)
    for_sibling(0, 4)
    for_me(0, 4)
    send_direct(0)
    for_sibling(0, 6)
    for_me(0, 6)
    for_sibling(1, 0, 2, 4, 6)
    send_far(0)
    for_me(1, 0, 2)
    send_corner(1)
    send_partner(0)
    send_other(1)
    for_me(1, 4, 6)
    send_merged(0)
    send_far(1)
    send_direct(1)
    send_partner(1)
    give_back(0)
    send_merged(1)
    give_back(1)

    most = pl.ds(0, owners - 1)
    for copy in gain_copies + sends + list(core_copies.values()) + moved:
        copy.wait_send()
    for part in range(PARTS):
        sent = out_buf.at[part, most]
        pltpu.make_async_copy(sent, sent, disp_send.at[part]).wait()

    for part in range(PARTS):
        pltpu.make_async_copy(ret_in.at[part], ret_in.at[part], ret_recv.at[part]).wait()
        for p in range(2):
            sides = [
                ret_in[part, (p * 2 + c) * experts_n : (p * 2 + c + 1) * experts_n].reshape(
                    experts_n * CAP, LANES
                )
                for c in range(2)
            ]
            start = p * quarter // 2 + part * both
            out_ref[:, start : start + both] = dot(
                take_t[...], jnp.concatenate(sides, axis=1)
            ).astype(BF16)
    for part in range(PARTS):
        sent = ret_out.at[part, most]
        pltpu.make_async_copy(sent, sent, ret_send.at[part]).wait()


def per_device(tokens, norm_gain, router, w_gate, w_up, w_down, picked):
    tok_dev, quarter = tokens.shape
    experts_n, capacity = picked.shape
    owners = lax.axis_size("expert")
    hid = w_gate.shape[2]
    width = 4 * quarter
    half = capacity // 2
    slots = experts_n * CAP
    dma = pltpu.SemaphoreType.DMA
    vmem = pl.BlockSpec(memory_space=pltpu.VMEM)
    hbm = pl.BlockSpec(memory_space=pl.ANY)
    return pl.pallas_call(
        functools.partial(kernel, owners),
        out_shape=jax.ShapeDtypeStruct((tok_dev, quarter), BF16),
        in_specs=[hbm] * 7,
        out_specs=vmem,
        scratch_shapes=[
            pltpu.VMEM((tok_dev, quarter), BF16),
            pltpu.VMEM((quarter // LANES, LANES), BF16),
            pltpu.VMEM((experts_n, width), BF16),
            pltpu.VMEM((experts_n, capacity), jnp.int32),
            pltpu.VMEM((width, 2 * hid + LANES), BF16),
            pltpu.VMEM((2, hid, width // 2), BF16),
            pltpu.VMEM((4, 16, LANES), BF16),
            pltpu.VMEM((32, LANES), F32),
            pltpu.VMEM((2, experts_n, capacity), F32),
            pltpu.VMEM((slots, LANES), F32),
            pltpu.VMEM((slots, tok_dev), BF16),
            pltpu.VMEM((tok_dev, slots), BF16),
            pltpu.VMEM((capacity, owners * CAP), BF16),
            pltpu.VMEM((owners * CAP, capacity), BF16),
            pltpu.VMEM((PARTS, owners, CAP, LANES), BF16),
            pltpu.VMEM((PARTS, owners, CAP, LANES), BF16),
            pltpu.VMEM((PARTS, 8, 2, capacity, LANES), BF16),
            pltpu.VMEM((capacity, 2 * hid + LANES), F32),
            pltpu.VMEM((capacity, LANES), F32),
            pltpu.VMEM((capacity, hid), BF16),
            pltpu.VMEM((capacity, LANES), F32),
            pltpu.VMEM((PARTS, 8, capacity, LANES), BF16),
            pltpu.VMEM((PARTS, 8, capacity, LANES), BF16),
            pltpu.VMEM((PARTS, 8, capacity, LANES), F32),
            pltpu.VMEM((PARTS, 2, 5, half, LANES), BF16),
            pltpu.VMEM((PARTS, 2, 5, half, LANES), BF16),
            pltpu.VMEM((PARTS, 4, half, LANES), BF16),
            pltpu.VMEM((PARTS, 4, half, LANES), BF16),
            pltpu.VMEM((PARTS, owners, CAP, LANES), BF16),
            pltpu.VMEM((PARTS, owners, CAP, LANES), BF16),
            dma((4,)),
            dma((3,)),
            dma((3,)),
            dma((4,)),
            dma((PARTS,)),
            dma((PARTS,)),
            dma((60,)),
            dma((64,)),
            dma((16,)),
            dma((16,)),
            dma((20,)),
            dma((20,)),
            dma((8,)),
            dma((8,)),
            dma((PARTS,)),
            dma((PARTS,)),
        ],
        compiler_params=pltpu.CompilerParams(
            collective_id=0, has_side_effects=True, vmem_limit_bytes=56 * 1024 * 1024
        ),
        cost_estimate=pl.CostEstimate(
            flops=2 * capacity * width * 3 * hid,
            bytes_accessed=3 * 2 * width * hid + 4 * tok_dev * quarter,
            transcendentals=capacity * hid,
        ),
    )(
        tokens,
        norm_gain.reshape(quarter // LANES, LANES),
        router.T,
        w_gate,
        w_up,
        w_down,
        picked,
    )


def solution(mesh):
    return jax.shard_map(
        per_device,
        mesh=mesh,
        in_specs=(
            P("expert", "mp"),
            P("mp"),
            P(),
            P("expert", None, "mp"),
            P("expert", None, "mp"),
            P("expert", "mp", None),
            P(),
        ),
        out_specs=P("expert", "mp"),
        check_vma=False,
    )
```

```python
import functools

import jax
import jax.numpy as jnp
from jax import lax
from jax.experimental import pallas as pl
from jax.experimental.pallas import tpu as pltpu
from jax.sharding import PartitionSpec as P

SLICES = 4
CAP = 16
PARTS = 2
LANES = 128
EPS = 1e-06
MESH = pl.DeviceIdType.MESH
F32 = jnp.float32
BF16 = jnp.bfloat16


def remote(src, dst, send, recv, device):
    return pltpu.make_async_remote_copy(
        src_ref=src,
        dst_ref=dst,
        send_sem=send,
        recv_sem=recv,
        device_id=device,
        device_id_type=MESH,
    )


def dot(lhs, rhs):
    return jnp.dot(lhs, rhs, preferred_element_type=F32)


def one_hot(condition):
    return jnp.where(condition, 1.0, 0.0).astype(BF16)


def iota(shape, dim):
    return lax.broadcasted_iota(jnp.int32, shape, dim).astype(F32)


def kernel(
    owners,
    tokens_hbm,
    gain_hbm,
    router_hbm,
    wg_ref,
    wu_ref,
    wd_ref,
    picked_hbm,
    ret_in,
    take_hbm,
    tokens_ref,
    gain_ref,
    router_ref,
    picked_ref,
    w_cat,
    w_down,
    gains,
    gains_f,
    ranked,
    chosen_tok,
    take,
    take_t,
    place,
    place_t,
    out_buf,
    in_buf,
    rows,
    acc,
    squares,
    hidden,
    gate,
    core_out,
    core_in,
    keep,
    y_out,
    y_in,
    x_out,
    x_in,
    ret_out,
    in_sem,
    take_sem,
    w_sem,
    gain_send,
    gain_recv,
    disp_send,
    disp_recv,
    ag_send,
    ag_recv,
    core_send,
    core_recv,
    y_send,
    y_recv,
    x_send,
    x_recv,
    ret_send,
    ret_recv,
):
    tok_dev, quarter = tokens_ref.shape
    experts_n, capacity = picked_ref.shape
    hid = wg_ref.shape[2]
    width = 4 * quarter
    half = capacity // 2
    both = 2 * LANES
    me = lax.axis_index("expert")
    y = lax.axis_index("mp")
    core = lax.rem(me, 2)
    pair = lax.rem(me // 2, 2)
    other = 1 - pair
    my_slice = lax.rem(me, SLICES)
    my_expert = me // SLICES
    sib = (me + 1 - 2 * core, y)
    xpart = (me + 2 - 4 * pair, y)
    y_up = lax.rem(y + 1, 4)
    y_down = lax.rem(y + 3, 4)
    y_far = lax.rem(y + 2, 4)
    up, down = (me, y_up), (me, y_down)

    def peer(r):
        return (lax.rem(me + r, owners), y)

    barrier = pltpu.get_barrier_semaphore()

    def greet(r, carry):
        pl.semaphore_signal(barrier, inc=1, device_id=peer(r), device_id_type=MESH)
        return carry

    for r in range(1, 4):
        pl.semaphore_signal(
            barrier, inc=1, device_id=(me, lax.rem(y + r, 4)), device_id_type=MESH
        )
    lax.fori_loop(1, owners, greet, 0)

    in_copies = [
        pltpu.make_async_copy(src, dst, in_sem.at[k])
        for k, (src, dst) in enumerate(
            [
                (picked_hbm, picked_ref),
                (tokens_hbm, tokens_ref),
                (gain_hbm, gain_ref),
                (router_hbm, router_ref),
            ]
        )
    ]
    w_copies = [
        pltpu.make_async_copy(wg_ref.at[0], w_cat.at[:, pl.ds(0, hid)], w_sem.at[0]),
        pltpu.make_async_copy(wu_ref.at[0], w_cat.at[:, pl.ds(hid, hid)], w_sem.at[1]),
    ]
    for copy in in_copies + w_copies:
        copy.start()

    tri = one_hot(iota((capacity, capacity), 0) <= iota((capacity, capacity), 1))
    in_copies[0].wait()
    rel = picked_ref[...] - me * tok_dev
    mine = jnp.where((rel >= 0) & (rel < tok_dev), 1.0, 0.0)
    ranked[0] = dot(mine.astype(BF16), tri) * mine
    ranked[1] = rel.astype(F32) + 1.0
    slot_no = iota((CAP, capacity), 0) + 1.0
    lane_no = iota((CAP, tok_dev), 1)
    for e in range(experts_n):
        hit = ranked[0, e : e + 1, :] == slot_no
        found = jnp.where(hit, ranked[1, e : e + 1, :], 0.0)
        token = jnp.sum(found, axis=1, keepdims=True) - 1.0
        take[e * CAP : (e + 1) * CAP, :] = one_hot(token == lane_no)
        chosen_tok[e * CAP : (e + 1) * CAP, :] = jnp.broadcast_to(token, (CAP, LANES))

    row = picked_ref[pl.ds(my_expert, 1), :]
    low = lax.broadcasted_iota(jnp.int32, (owners, capacity), 0) * tok_dev
    held = jnp.where((row >= low) & (row < low + tok_dev), 1.0, 0.0)
    slot_at = dot(held.astype(BF16), tri) - 1.0 + iota((owners, capacity), 0) * CAP
    flat = jnp.sum(held * slot_at, axis=0, keepdims=True)
    flat_col = jnp.broadcast_to(flat, (LANES, capacity)).T
    down_no = iota((LANES, capacity), 0)
    across_no = iota((capacity, LANES), 1)
    for j in range(owners * CAP // LANES):
        span = slice(j * LANES, (j + 1) * LANES)
        place_t[span, :] = one_hot(flat == down_no + j * LANES)
        place[:, span] = one_hot(flat_col == across_no + j * LANES)
    take_t[...] = one_hot(chosen_tok[...].T[0:1, :] == iota((tok_dev, experts_n * CAP), 0))
    take_copy = pltpu.make_async_copy(take_t, take_hbm, take_sem.at[0])
    take_copy.start()

    def gather(part):
        for p in range(2):
            start = p * quarter // 2 + part * both
            found = dot(take[...], tokens_ref[:, start : start + both]).astype(BF16)
            for e in range(experts_n):
                for c in range(2):
                    out_buf[part, e * SLICES + p * 2 + c] = found[
                        e * CAP : (e + 1) * CAP, c * LANES : (c + 1) * LANES
                    ]

    in_copies[1].wait()
    gather(0)
    gather(1)
    in_copies[2].wait()
    in_copies[3].wait()
    select = one_hot(iota((experts_n, LANES), 0) == my_expert.astype(F32))
    for j in range(8):
        span = slice(j * width // 8, (j + 1) * width // 8)
        w_cat[span, 2 * hid :] = lax.dot_general(
            router_ref[:, span],
            select,
            (((0,), (0,)), ((), ())),
            preferred_element_type=F32,
        ).astype(BF16)
    gains[y] = jnp.concatenate([gain_ref[...], gain_ref[...]], axis=0)

    pl.semaphore_wait(barrier, owners - 1 + 3)

    targets = [
        (y_far, other),
        (y_up, other),
        (y_down, other),
        (y_far, pair),
        (y_up, pair),
        (y_down, pair),
        (y, other),
        (y, pair),
    ]

    def load_down():
        for part in range(PARTS):
            for k, (at_y, at_pair) in enumerate(targets):
                for side, c in enumerate((core, 1 - core)):
                    start = at_y * quarter + at_pair * (quarter // 2) + part * both + c * LANES
                    pltpu.make_async_copy(
                        wd_ref.at[0, :, pl.ds(pl.multiple_of(start, LANES), LANES)],
                        w_down.at[side, :, pl.ds((part * 8 + k) * LANES, LANES)],
                        w_sem.at[2],
                    ).start()

    def dispatch(part):
        for side in range(2):

            def start(j, carry):
                d = 2 * lax.rem(me // 2 + j, owners // 2) + side
                remote(
                    out_buf.at[part, d],
                    in_buf.at[part, me],
                    disp_send.at[part],
                    disp_recv.at[part],
                    (d, y),
                ).start()
                return carry

            first = 1 - core if side == 0 else core
            lax.fori_loop(first, owners // 2, start, 0)
        pltpu.make_async_copy(
            out_buf.at[part, me], in_buf.at[part, me], disp_recv.at[part]
        ).start()

    gain_copies = []
    for r in range(1, 4):
        copy = remote(
            gains.at[y],
            gains.at[y],
            gain_send.at[r - 1],
            gain_recv.at[y],
            (me, lax.rem(y + r, 4)),
        )
        copy.start()
        gain_copies.append(copy)
    dispatch(0)
    dispatch(1)
    load_down()

    for r in range(1, 4):
        at = lax.rem(y + r, 4)
        remote(gains.at[at], gains.at[at], gain_send.at[0], gain_recv.at[at], up).wait_recv()
    for at in range(4):
        gains_f[at * 8 : (at + 1) * 8, :] = gains[at][:8, :].astype(F32)
    w_copies[0].wait()
    w_copies[1].wait()

    def scale(q, carry):
        start = pl.multiple_of(q * LANES, LANES)
        column = jnp.broadcast_to(gains_f[pl.ds(q, 1), :], (LANES, LANES)).T
        for j in range(2 * hid // LANES + 1):
            cols = slice(j * LANES, (j + 1) * LANES)
            w_cat[pl.ds(start, LANES), cols] = (
                w_cat[pl.ds(start, LANES), cols].astype(F32) * column
            ).astype(BF16)
        return carry

    lax.fori_loop(0, width // LANES, scale, 0, unroll=4)

    def block(at_y, at_pair):
        return at_y * 2 + at_pair

    def ag(part, b, c, h, k, device):
        at = rows.at[part, b, c, pl.ds(h * half, half)]
        number = ((part * 8 + b) * 2 + c) * 2 + h
        return remote(at, at, ag_send.at[k], ag_recv.at[number], device)

    sends = []

    def go(part, b, h, *devices):
        for device in devices:
            copy = ag(part, b, core, h, len(sends), device)
            copy.start()
            sends.append(copy)

    def pass_on(part, b, h, *devices):
        ag(part, b, core, h, 0, sib).wait_recv()
        go(part, b, h, *devices, sib)

    def begin(part):
        pltpu.make_async_copy(in_buf.at[part], in_buf.at[part], disp_recv.at[part]).wait()
        b = block(y, pair)
        rows[part, b, core] = dot(
            place[...], in_buf[part].reshape(owners * CAP, LANES)
        ).astype(BF16)
        for h in range(2):
            go(part, b, h, xpart, up)
            go(part, b, 1 - h, down)
            go(part, b, h, sib)

    def from_neighbours(part):
        pass_on(part, block(y_down, pair), 0, up)
        pass_on(part, block(y_up, pair), 1, down)

    def rest_of_neighbours(part):
        pass_on(part, block(y_down, pair), 1)
        pass_on(part, block(y_up, pair), 0)

    def from_partner(part, h):
        pass_on(part, block(y, other), h, up, down)

    def from_far(part):
        for h in range(2):
            pass_on(part, block(y_far, pair), h, xpart)

    def from_corners(part):
        for h in range(2):
            pass_on(part, block(y_down, other), h)
            pass_on(part, block(y_up, other), h)

    def from_far_corner(part):
        for h in range(2):
            pass_on(part, block(y_far, other), h)

    def product(part, at_y, at_pair, first=False):
        b = block(at_y, at_pair)
        for h in range(2):
            ag(part, b, 1 - core, h, 0, sib).wait_recv()
        start = pl.multiple_of(
            at_y * quarter + at_pair * (quarter // 2) + part * both, both
        )
        left, right = rows[part, b, 0], rows[part, b, 1]
        new = dot(jnp.concatenate([left, right], axis=1), w_cat[pl.ds(start, both), :])
        left, right = left.astype(F32), right.astype(F32)
        square = left * left + right * right
        if first:
            acc[...] = new
            squares[...] = square
        else:
            acc[...] += new
            squares[...] += square

    begin(0)
    from_neighbours(0)
    from_partner(0, 0)
    begin(1)
    from_partner(0, 1)
    rest_of_neighbours(0)
    product(0, y, pair, first=True)
    product(0, y_down, pair)
    from_far(0)
    product(0, y_up, pair)
    from_neighbours(1)
    from_partner(1, 0)
    from_partner(1, 1)
    rest_of_neighbours(1)
    product(0, y, other)
    product(1, y, pair)
    product(0, y_far, pair)
    from_corners(0)
    product(1, y_down, pair)
    from_far(1)
    product(1, y_up, pair)
    product(1, y, other)
    from_far_corner(0)
    product(0, y_down, other)
    product(0, y_up, other)
    product(0, y_far, other)
    from_corners(1)
    product(1, y_far, pair)
    product(1, y_down, other)
    product(1, y_up, other)
    from_far_corner(1)
    product(1, y_far, other)

    total = jnp.sum(squares[...], axis=1, keepdims=True)
    inv = lax.rsqrt(total * (1.0 / width) + EPS)
    hidden[...] = (
        jax.nn.gelu(acc[:, :hid] * inv, approximate=True) * (acc[:, hid : 2 * hid] * inv)
    ).astype(BF16)
    gate[...] = jax.nn.sigmoid(acc[:, 2 * hid :] * inv).astype(BF16).astype(F32)
    pltpu.make_async_copy(w_down, w_down, w_sem.at[2]).wait()

    top, bottom = slice(0, half), slice(half, capacity)
    core_copies = {}

    def partial(part, k, side):
        start = (part * 8 + k) * LANES
        return dot(hidden[...], w_down[side, :, start : start + both])

    def for_sibling(part, *firsts):
        for first in firsts:
            value = partial(part, first, 1)
            for k in (first, first + 1):
                at = (k - first) * LANES
                core_out[part, k] = value[:, at : at + LANES].astype(BF16)
                number = part * 8 + k
                copy = remote(
                    core_out.at[part, k],
                    core_in.at[part, k],
                    core_send.at[number],
                    core_recv.at[number],
                    sib,
                )
                copy.start()
                core_copies[part, k] = copy

    def for_me(part, *firsts):
        for first in firsts:
            value = partial(part, first, 0)
            keep[part, first] = value[:, :LANES]
            keep[part, first + 1] = value[:, LANES:]

    def chip(part, k):
        core_copies[part, k].wait_recv()
        return keep[part, k] + core_in[part, k].astype(F32)

    moved = []

    def y_copy(part, way, m):
        number = (part * 2 + way) * 5 + m
        return remote(
            y_out.at[part, way, m],
            y_in.at[part, way, m],
            y_send.at[number],
            y_recv.at[number],
            (up, down)[way],
        )

    def y_go(part, way, m, value):
        y_out[part, way, m] = value.astype(BF16)
        copy = y_copy(part, way, m)
        copy.start()
        moved.append(copy)

    def y_got(part, way, m):
        y_copy(part, way, m).wait_recv()
        return y_in[part, way, m].astype(F32)

    def x_copy(part, m):
        number = part * 4 + m
        return remote(
            x_out.at[part, m], x_in.at[part, m], x_send.at[number], x_recv.at[number], xpart
        )

    def x_go(part, m, value):
        x_out[part, m] = value.astype(BF16)
        copy = x_copy(part, m)
        copy.start()
        moved.append(copy)

    def x_got(part, m):
        x_copy(part, m).wait_recv()
        return x_in[part, m].astype(F32)

    def send_corner(part):
        value = chip(part, 0)
        x_go(part, 0, value[top])
        x_go(part, 1, value[bottom])

    def send_other(part):
        for way in range(2):
            value = chip(part, 1 + way)
            y_go(part, way, 0, value[top])
            y_go(part, way, 1, value[bottom])

    def send_direct(part):
        value = chip(part, 4)
        y_go(part, 0, 2, value[top])
        keep[part, 4, bottom] = value[bottom]
        value = chip(part, 5)
        y_go(part, 1, 2, value[bottom])
        keep[part, 5, top] = value[top]

    def send_far(part):
        value = chip(part, 3)
        y_go(part, 1, 3, value[top] + x_got(part, 0))
        y_go(part, 0, 3, value[bottom] + x_got(part, 1))

    def send_merged(part):
        y_go(part, 1, 4, keep[part, 5, top] + y_got(part, 1, 3))
        y_go(part, 0, 4, keep[part, 4, bottom] + y_got(part, 0, 3))

    def send_partner(part):
        value = chip(part, 6)
        x_go(part, 2, value[top] + y_got(part, 0, 0) + y_got(part, 1, 0))
        x_go(part, 3, value[bottom] + y_got(part, 0, 1) + y_got(part, 1, 1))

    back = my_slice * experts_n + my_expert

    def give_back(part):
        value = chip(part, 7)
        upper = value[top] + y_got(part, 0, 2) + y_got(part, 1, 4) + x_got(part, 2)
        lower = value[bottom] + y_got(part, 1, 2) + y_got(part, 0, 4) + x_got(part, 3)
        gated = (jnp.concatenate([upper, lower], axis=0) * gate[...]).astype(BF16)
        ret_out[part] = dot(place_t[...], gated).astype(BF16).reshape(owners, CAP, LANES)

        def start(r, carry):
            d, _ = peer(r)
            remote(
                ret_out.at[part, d],
                ret_in.at[part, back],
                ret_send.at[part],
                ret_recv.at[part],
                (d, y),
            ).start()
            return carry

        lax.fori_loop(1, owners, start, 0)
        pltpu.make_async_copy(
            ret_out.at[part, me], ret_in.at[part, back], ret_recv.at[part]
        ).start()

    for_sibling(0, 0, 2)
    for_me(0, 0)
    send_corner(0)
    for_me(0, 2)
    send_other(0)
    for_sibling(0, 4)
    for_me(0, 4)
    send_direct(0)
    for_sibling(0, 6)
    for_me(0, 6)
    for_sibling(1, 0, 2, 4, 6)
    send_far(0)
    for_me(1, 0, 2)
    send_corner(1)
    send_partner(0)
    send_other(1)
    for_me(1, 4, 6)
    send_merged(0)
    send_far(1)
    send_direct(1)
    send_partner(1)
    give_back(0)
    send_merged(1)
    give_back(1)

    most = pl.ds(0, owners - 1)
    for copy in gain_copies + sends + list(core_copies.values()) + moved:
        copy.wait_send()
    for part in range(PARTS):
        sent = out_buf.at[part, most]
        pltpu.make_async_copy(sent, sent, disp_send.at[part]).wait()

    take_copy.wait()
    for part in range(PARTS):
        sent = ret_out.at[part, most]
        pltpu.make_async_copy(ret_in.at[part], ret_in.at[part], ret_recv.at[part]).wait()
        pltpu.make_async_copy(sent, sent, ret_send.at[part]).wait()


def add_up(ret_hbm, take_hbm, out_hbm, ret, take_t, out, in_sem, out_sem):
    slots = take_t.shape[1]
    experts_n = slots // CAP
    both = 2 * LANES
    take_copy = pltpu.make_async_copy(take_hbm, take_t, in_sem.at[PARTS])
    copies = [
        pltpu.make_async_copy(ret_hbm.at[part], ret.at[part], in_sem.at[part])
        for part in range(PARTS)
    ]
    take_copy.start()
    for copy in copies:
        copy.start()
    take_copy.wait()
    out_copies = []
    for part in range(PARTS):
        copies[part].wait()
        for p in range(2):
            sides = [
                ret[part, (p * 2 + c) * experts_n : (p * 2 + c + 1) * experts_n].reshape(
                    slots, LANES
                )
                for c in range(2)
            ]
            k = part * 2 + p
            out[k] = dot(take_t[...], jnp.concatenate(sides, axis=1)).astype(BF16)
            start = p * (PARTS * both) + part * both
            copy = pltpu.make_async_copy(
                out.at[k], out_hbm.at[:, pl.ds(start, both)], out_sem.at[k]
            )
            copy.start()
            out_copies.append(copy)
    for copy in out_copies:
        copy.wait()


def per_device(tokens, norm_gain, router, w_gate, w_up, w_down, picked):
    tok_dev, quarter = tokens.shape
    experts_n, capacity = picked.shape
    owners = lax.axis_size("expert")
    hid = w_gate.shape[2]
    width = 4 * quarter
    half = capacity // 2
    slots = experts_n * CAP
    dma = pltpu.SemaphoreType.DMA
    hbm = pl.BlockSpec(memory_space=pl.ANY)
    returned, take_t = pl.pallas_call(
        functools.partial(kernel, owners),
        out_shape=(
            jax.ShapeDtypeStruct((PARTS, owners, CAP, LANES), BF16),
            jax.ShapeDtypeStruct((tok_dev, slots), BF16),
        ),
        in_specs=[hbm] * 7,
        out_specs=(hbm, hbm),
        scratch_shapes=[
            pltpu.VMEM((tok_dev, quarter), BF16),
            pltpu.VMEM((quarter // LANES, LANES), BF16),
            pltpu.VMEM((experts_n, width), BF16),
            pltpu.VMEM((experts_n, capacity), jnp.int32),
            pltpu.VMEM((width, 2 * hid + LANES), BF16),
            pltpu.VMEM((2, hid, width // 2), BF16),
            pltpu.VMEM((4, 16, LANES), BF16),
            pltpu.VMEM((32, LANES), F32),
            pltpu.VMEM((2, experts_n, capacity), F32),
            pltpu.VMEM((slots, LANES), F32),
            pltpu.VMEM((slots, tok_dev), BF16),
            pltpu.VMEM((tok_dev, slots), BF16),
            pltpu.VMEM((capacity, owners * CAP), BF16),
            pltpu.VMEM((owners * CAP, capacity), BF16),
            pltpu.VMEM((PARTS, owners, CAP, LANES), BF16),
            pltpu.VMEM((PARTS, owners, CAP, LANES), BF16),
            pltpu.VMEM((PARTS, 8, 2, capacity, LANES), BF16),
            pltpu.VMEM((capacity, 2 * hid + LANES), F32),
            pltpu.VMEM((capacity, LANES), F32),
            pltpu.VMEM((capacity, hid), BF16),
            pltpu.VMEM((capacity, LANES), F32),
            pltpu.VMEM((PARTS, 8, capacity, LANES), BF16),
            pltpu.VMEM((PARTS, 8, capacity, LANES), BF16),
            pltpu.VMEM((PARTS, 8, capacity, LANES), F32),
            pltpu.VMEM((PARTS, 2, 5, half, LANES), BF16),
            pltpu.VMEM((PARTS, 2, 5, half, LANES), BF16),
            pltpu.VMEM((PARTS, 4, half, LANES), BF16),
            pltpu.VMEM((PARTS, 4, half, LANES), BF16),
            pltpu.VMEM((PARTS, owners, CAP, LANES), BF16),
            dma((4,)),
            dma((1,)),
            dma((3,)),
            dma((3,)),
            dma((4,)),
            dma((PARTS,)),
            dma((PARTS,)),
            dma((60,)),
            dma((64,)),
            dma((16,)),
            dma((16,)),
            dma((20,)),
            dma((20,)),
            dma((8,)),
            dma((8,)),
            dma((PARTS,)),
            dma((PARTS,)),
        ],
        compiler_params=pltpu.CompilerParams(
            collective_id=0, has_side_effects=True, vmem_limit_bytes=56 * 1024 * 1024
        ),
        cost_estimate=pl.CostEstimate(
            flops=2 * capacity * width * 3 * hid,
            bytes_accessed=3 * 2 * width * hid + 4 * tok_dev * quarter,
            transcendentals=capacity * hid,
        ),
    )(
        tokens,
        norm_gain.reshape(quarter // LANES, LANES),
        router.T,
        w_gate,
        w_up,
        w_down,
        picked,
    )
    return pl.pallas_call(
        add_up,
        out_shape=jax.ShapeDtypeStruct((tok_dev, quarter), BF16),
        in_specs=[hbm, hbm],
        out_specs=hbm,
        scratch_shapes=[
            pltpu.VMEM((PARTS, owners, CAP, LANES), BF16),
            pltpu.VMEM((tok_dev, slots), BF16),
            pltpu.VMEM((2 * PARTS, tok_dev, 2 * LANES), BF16),
            dma((PARTS + 1,)),
            dma((2 * PARTS,)),
        ],
        compiler_params=pltpu.CompilerParams(vmem_limit_bytes=56 * 1024 * 1024),
        cost_estimate=pl.CostEstimate(
            flops=2 * tok_dev * slots * quarter,
            bytes_accessed=2 * (2 * slots + tok_dev) * quarter,
            transcendentals=0,
        ),
    )(returned, take_t)


def solution(mesh):
    return jax.shard_map(
        per_device,
        mesh=mesh,
        in_specs=(
            P("expert", "mp"),
            P("mp"),
            P(),
            P("expert", None, "mp"),
            P("expert", None, "mp"),
            P("expert", "mp", None),
            P(),
        ),
        out_specs=P("expert", "mp"),
        check_vma=False,
    )
```

```python
import functools

import jax
import jax.numpy as jnp
from jax import lax
from jax.experimental import pallas as pl
from jax.experimental.pallas import tpu as pltpu
from jax.sharding import PartitionSpec as P

SLICES = 4
CAP = 16
PARTS = 2
LANES = 128
EPS = 1e-06
MESH = pl.DeviceIdType.MESH
F32 = jnp.float32
BF16 = jnp.bfloat16


def remote(src, dst, send, recv, device):
    return pltpu.make_async_remote_copy(
        src_ref=src,
        dst_ref=dst,
        send_sem=send,
        recv_sem=recv,
        device_id=device,
        device_id_type=MESH,
    )


def dot(lhs, rhs):
    return jnp.dot(lhs, rhs, preferred_element_type=F32)


def one_hot(condition):
    return jnp.where(condition, 1.0, 0.0).astype(BF16)


def iota(shape, dim):
    return lax.broadcasted_iota(jnp.int32, shape, dim).astype(F32)


def kernel(
    owners,
    tokens_hbm,
    gain_hbm,
    router_hbm,
    wg_ref,
    wu_ref,
    wd_ref,
    picked_hbm,
    ret_in,
    take_hbm,
    tokens_ref,
    gain_ref,
    router_ref,
    picked_ref,
    w_cat,
    w_down,
    gains,
    gains_f,
    ranked,
    chosen_tok,
    take,
    take_t,
    place,
    place_t,
    out_buf,
    in_buf,
    rows,
    acc,
    squares,
    hidden,
    gate,
    core_out,
    core_in,
    keep,
    y_out,
    y_in,
    x_out,
    x_in,
    ret_out,
    in_sem,
    take_sem,
    w_sem,
    gain_send,
    gain_recv,
    disp_send,
    disp_recv,
    ag_send,
    ag_recv,
    core_send,
    core_recv,
    y_send,
    y_recv,
    x_send,
    x_recv,
    ret_send,
    ret_recv,
):
    tok_dev, quarter = tokens_ref.shape
    experts_n, capacity = picked_ref.shape
    hid = wg_ref.shape[2]
    width = 4 * quarter
    half = capacity // 2
    both = 2 * LANES
    me = lax.axis_index("expert")
    y = lax.axis_index("mp")
    core = lax.rem(me, 2)
    pair = lax.rem(me // 2, 2)
    other = 1 - pair
    my_slice = lax.rem(me, SLICES)
    my_expert = me // SLICES
    sib = (me + 1 - 2 * core, y)
    xpart = (me + 2 - 4 * pair, y)
    y_up = lax.rem(y + 1, 4)
    y_down = lax.rem(y + 3, 4)
    y_far = lax.rem(y + 2, 4)
    up, down = (me, y_up), (me, y_down)

    def peer(r):
        return (lax.rem(me + r, owners), y)

    barrier = pltpu.get_barrier_semaphore()

    def greet(r, carry):
        pl.semaphore_signal(barrier, inc=1, device_id=peer(r), device_id_type=MESH)
        return carry

    for r in range(1, 4):
        pl.semaphore_signal(
            barrier, inc=1, device_id=(me, lax.rem(y + r, 4)), device_id_type=MESH
        )
    lax.fori_loop(1, owners, greet, 0)

    in_copies = [
        pltpu.make_async_copy(src, dst, in_sem.at[k])
        for k, (src, dst) in enumerate(
            [
                (picked_hbm, picked_ref),
                (tokens_hbm, tokens_ref),
                (gain_hbm, gain_ref),
                (router_hbm, router_ref),
            ]
        )
    ]
    w_copies = [
        pltpu.make_async_copy(wg_ref.at[0], w_cat.at[:, pl.ds(0, hid)], w_sem.at[0]),
        pltpu.make_async_copy(wu_ref.at[0], w_cat.at[:, pl.ds(hid, hid)], w_sem.at[1]),
    ]
    for copy in in_copies + w_copies:
        copy.start()

    tri = one_hot(iota((capacity, capacity), 0) <= iota((capacity, capacity), 1))
    in_copies[0].wait()
    rel = picked_ref[...] - me * tok_dev
    mine = jnp.where((rel >= 0) & (rel < tok_dev), 1.0, 0.0)
    ranked[0] = dot(mine.astype(BF16), tri) * mine
    ranked[1] = rel.astype(F32) + 1.0
    slot_no = iota((CAP, capacity), 0) + 1.0
    lane_no = iota((CAP, tok_dev), 1)
    for e in range(experts_n):
        hit = ranked[0, e : e + 1, :] == slot_no
        found = jnp.where(hit, ranked[1, e : e + 1, :], 0.0)
        token = jnp.sum(found, axis=1, keepdims=True) - 1.0
        take[e * CAP : (e + 1) * CAP, :] = one_hot(token == lane_no)
        chosen_tok[e * CAP : (e + 1) * CAP, :] = jnp.broadcast_to(token, (CAP, LANES))

    row = picked_ref[pl.ds(my_expert, 1), :]
    low = lax.broadcasted_iota(jnp.int32, (owners, capacity), 0) * tok_dev
    held = jnp.where((row >= low) & (row < low + tok_dev), 1.0, 0.0)
    slot_at = dot(held.astype(BF16), tri) - 1.0 + iota((owners, capacity), 0) * CAP
    flat = jnp.sum(held * slot_at, axis=0, keepdims=True)
    flat_col = jnp.broadcast_to(flat, (LANES, capacity)).T
    down_no = iota((LANES, capacity), 0)
    across_no = iota((capacity, LANES), 1)
    for j in range(owners * CAP // LANES):
        span = slice(j * LANES, (j + 1) * LANES)
        place_t[span, :] = one_hot(flat == down_no + j * LANES)
        place[:, span] = one_hot(flat_col == across_no + j * LANES)
    take_t[...] = one_hot(chosen_tok[...].T[0:1, :] == iota((tok_dev, experts_n * CAP), 0))
    take_copy = pltpu.make_async_copy(take_t, take_hbm, take_sem.at[0])
    take_copy.start()

    def gather(part):
        for p in range(2):
            start = p * quarter // 2 + part * both
            found = dot(take[...], tokens_ref[:, start : start + both]).astype(BF16)
            for e in range(experts_n):
                for c in range(2):
                    out_buf[part, e * SLICES + p * 2 + c] = found[
                        e * CAP : (e + 1) * CAP, c * LANES : (c + 1) * LANES
                    ]

    in_copies[1].wait()
    gather(0)
    gather(1)
    in_copies[2].wait()
    in_copies[3].wait()
    select = one_hot(iota((experts_n, LANES), 0) == my_expert.astype(F32))
    for j in range(8):
        span = slice(j * width // 8, (j + 1) * width // 8)
        w_cat[span, 2 * hid :] = lax.dot_general(
            router_ref[:, span],
            select,
            (((0,), (0,)), ((), ())),
            preferred_element_type=F32,
        ).astype(BF16)
    gains[y] = jnp.concatenate([gain_ref[...], gain_ref[...]], axis=0)

    pl.semaphore_wait(barrier, owners - 1 + 3)

    targets = [
        (y_far, other),
        (y_up, other),
        (y_down, other),
        (y_far, pair),
        (y_up, pair),
        (y_down, pair),
        (y, other),
        (y, pair),
    ]

    def load_down():
        for part in range(PARTS):
            for k, (at_y, at_pair) in enumerate(targets):
                for side, c in enumerate((core, 1 - core)):
                    start = at_y * quarter + at_pair * (quarter // 2) + part * both + c * LANES
                    pltpu.make_async_copy(
                        wd_ref.at[0, :, pl.ds(pl.multiple_of(start, LANES), LANES)],
                        w_down.at[side, :, pl.ds((part * 8 + k) * LANES, LANES)],
                        w_sem.at[2],
                    ).start()

    def dispatch(part):
        for side in range(2):

            def start(j, carry):
                d = 2 * lax.rem(me // 2 + j, owners // 2) + side
                remote(
                    out_buf.at[part, d],
                    in_buf.at[part, me],
                    disp_send.at[part],
                    disp_recv.at[part],
                    (d, y),
                ).start()
                return carry

            first = 1 - core if side == 0 else core
            lax.fori_loop(first, owners // 2, start, 0)
        pltpu.make_async_copy(
            out_buf.at[part, me], in_buf.at[part, me], disp_recv.at[part]
        ).start()

    gain_copies = []
    for r in range(1, 4):
        copy = remote(
            gains.at[y],
            gains.at[y],
            gain_send.at[r - 1],
            gain_recv.at[y],
            (me, lax.rem(y + r, 4)),
        )
        copy.start()
        gain_copies.append(copy)
    dispatch(0)
    dispatch(1)
    load_down()

    for r in range(1, 4):
        at = lax.rem(y + r, 4)
        remote(gains.at[at], gains.at[at], gain_send.at[0], gain_recv.at[at], up).wait_recv()
    for at in range(4):
        gains_f[at * 8 : (at + 1) * 8, :] = gains[at][:8, :].astype(F32)
    w_copies[0].wait()
    w_copies[1].wait()

    def scale(q, carry):
        start = pl.multiple_of(q * LANES, LANES)
        column = jnp.broadcast_to(gains_f[pl.ds(q, 1), :], (LANES, LANES)).T
        for j in range(2 * hid // LANES + 1):
            cols = slice(j * LANES, (j + 1) * LANES)
            w_cat[pl.ds(start, LANES), cols] = (
                w_cat[pl.ds(start, LANES), cols].astype(F32) * column
            ).astype(BF16)
        return carry

    lax.fori_loop(0, width // LANES, scale, 0, unroll=4)

    def block(at_y, at_pair):
        return at_y * 2 + at_pair

    def ag(part, b, c, h, k, device):
        at = rows.at[part, b, c, pl.ds(h * half, half)]
        number = ((part * 8 + b) * 2 + c) * 2 + h
        return remote(at, at, ag_send.at[k], ag_recv.at[number], device)

    sends = []

    def go(part, b, h, *devices):
        for device in devices:
            copy = ag(part, b, core, h, len(sends), device)
            copy.start()
            sends.append(copy)

    def pass_on(part, b, h, *devices):
        ag(part, b, core, h, 0, sib).wait_recv()
        go(part, b, h, *devices, sib)

    def begin(part):
        pltpu.make_async_copy(in_buf.at[part], in_buf.at[part], disp_recv.at[part]).wait()
        b = block(y, pair)
        rows[part, b, core] = dot(
            place[...], in_buf[part].reshape(owners * CAP, LANES)
        ).astype(BF16)
        for h in range(2):
            go(part, b, h, xpart, up)
            go(part, b, 1 - h, down)
            go(part, b, h, sib)

    def from_neighbours(part):
        pass_on(part, block(y_down, pair), 0, up)
        pass_on(part, block(y_up, pair), 1, down)

    def rest_of_neighbours(part):
        pass_on(part, block(y_down, pair), 1)
        pass_on(part, block(y_up, pair), 0)

    def from_partner(part, h):
        pass_on(part, block(y, other), h, up, down)

    def from_far(part):
        for h in range(2):
            pass_on(part, block(y_far, pair), h, xpart)

    def from_corners(part):
        for h in range(2):
            pass_on(part, block(y_down, other), h)
            pass_on(part, block(y_up, other), h)

    def from_far_corner(part):
        for h in range(2):
            pass_on(part, block(y_far, other), h)

    def product(part, at_y, at_pair, first=False):
        b = block(at_y, at_pair)
        for h in range(2):
            ag(part, b, 1 - core, h, 0, sib).wait_recv()
        start = pl.multiple_of(
            at_y * quarter + at_pair * (quarter // 2) + part * both, both
        )
        left, right = rows[part, b, 0], rows[part, b, 1]
        new = dot(jnp.concatenate([left, right], axis=1), w_cat[pl.ds(start, both), :])
        left, right = left.astype(F32), right.astype(F32)
        square = left * left + right * right
        if first:
            acc[...] = new
            squares[...] = square
        else:
            acc[...] += new
            squares[...] += square

    begin(0)
    from_neighbours(0)
    from_partner(0, 0)
    begin(1)
    from_neighbours(1)
    from_partner(0, 1)
    from_partner(1, 0)
    rest_of_neighbours(0)
    from_far(0)
    from_partner(1, 1)
    product(0, y, pair, first=True)
    product(0, y_down, pair)
    product(0, y_up, pair)
    rest_of_neighbours(1)
    from_far(1)
    product(0, y, other)
    product(1, y, pair)
    product(0, y_far, pair)
    from_corners(0)
    product(1, y_down, pair)
    product(1, y_up, pair)
    product(1, y, other)
    from_far_corner(0)
    product(0, y_down, other)
    product(0, y_up, other)
    product(0, y_far, other)
    from_corners(1)
    product(1, y_far, pair)
    product(1, y_down, other)
    product(1, y_up, other)
    from_far_corner(1)
    product(1, y_far, other)

    total = jnp.sum(squares[...], axis=1, keepdims=True)
    inv = lax.rsqrt(total * (1.0 / width) + EPS)
    hidden[...] = (
        jax.nn.gelu(acc[:, :hid] * inv, approximate=True) * (acc[:, hid : 2 * hid] * inv)
    ).astype(BF16)
    gate[...] = jax.nn.sigmoid(acc[:, 2 * hid :] * inv).astype(BF16).astype(F32)
    pltpu.make_async_copy(w_down, w_down, w_sem.at[2]).wait()

    top, bottom = slice(0, half), slice(half, capacity)
    core_copies = {}

    def partial(part, k, side):
        start = (part * 8 + k) * LANES
        return dot(hidden[...], w_down[side, :, start : start + both])

    def for_sibling(part, *firsts):
        for first in firsts:
            value = partial(part, first, 1)
            for k in (first, first + 1):
                at = (k - first) * LANES
                core_out[part, k] = value[:, at : at + LANES].astype(BF16)
                number = part * 8 + k
                copy = remote(
                    core_out.at[part, k],
                    core_in.at[part, k],
                    core_send.at[number],
                    core_recv.at[number],
                    sib,
                )
                copy.start()
                core_copies[part, k] = copy

    def for_me(part, *firsts):
        for first in firsts:
            value = partial(part, first, 0)
            keep[part, first] = value[:, :LANES]
            keep[part, first + 1] = value[:, LANES:]

    def chip(part, k):
        core_copies[part, k].wait_recv()
        return keep[part, k] + core_in[part, k].astype(F32)

    moved = []

    def y_copy(part, way, m):
        number = (part * 2 + way) * 5 + m
        return remote(
            y_out.at[part, way, m],
            y_in.at[part, way, m],
            y_send.at[number],
            y_recv.at[number],
            (up, down)[way],
        )

    def y_go(part, way, m, value):
        y_out[part, way, m] = value.astype(BF16)
        copy = y_copy(part, way, m)
        copy.start()
        moved.append(copy)

    def y_got(part, way, m):
        y_copy(part, way, m).wait_recv()
        return y_in[part, way, m].astype(F32)

    def x_copy(part, m):
        number = part * 4 + m
        return remote(
            x_out.at[part, m], x_in.at[part, m], x_send.at[number], x_recv.at[number], xpart
        )

    def x_go(part, m, value):
        x_out[part, m] = value.astype(BF16)
        copy = x_copy(part, m)
        copy.start()
        moved.append(copy)

    def x_got(part, m):
        x_copy(part, m).wait_recv()
        return x_in[part, m].astype(F32)

    def send_corner(part):
        value = chip(part, 0)
        x_go(part, 0, value[top])
        x_go(part, 1, value[bottom])

    def send_other(part):
        for way in range(2):
            value = chip(part, 1 + way)
            y_go(part, way, 0, value[top])
            y_go(part, way, 1, value[bottom])

    def send_direct(part):
        value = chip(part, 4)
        y_go(part, 0, 2, value[top])
        keep[part, 4, bottom] = value[bottom]
        value = chip(part, 5)
        y_go(part, 1, 2, value[bottom])
        keep[part, 5, top] = value[top]

    def send_far(part):
        value = chip(part, 3)
        y_go(part, 1, 3, value[top] + x_got(part, 0))
        y_go(part, 0, 3, value[bottom] + x_got(part, 1))

    def send_merged(part):
        y_go(part, 1, 4, keep[part, 5, top] + y_got(part, 1, 3))
        y_go(part, 0, 4, keep[part, 4, bottom] + y_got(part, 0, 3))

    def send_partner(part):
        value = chip(part, 6)
        x_go(part, 2, value[top] + y_got(part, 0, 0) + y_got(part, 1, 0))
        x_go(part, 3, value[bottom] + y_got(part, 0, 1) + y_got(part, 1, 1))

    back = my_slice * experts_n + my_expert

    def give_back(part):
        value = chip(part, 7)
        upper = value[top] + y_got(part, 0, 2) + y_got(part, 1, 4) + x_got(part, 2)
        lower = value[bottom] + y_got(part, 1, 2) + y_got(part, 0, 4) + x_got(part, 3)
        gated = (jnp.concatenate([upper, lower], axis=0) * gate[...]).astype(BF16)
        ret_out[part] = dot(place_t[...], gated).astype(BF16).reshape(owners, CAP, LANES)

        def start(r, carry):
            d, _ = peer(r)
            remote(
                ret_out.at[part, d],
                ret_in.at[part, back],
                ret_send.at[part],
                ret_recv.at[part],
                (d, y),
            ).start()
            return carry

        lax.fori_loop(1, owners, start, 0)
        pltpu.make_async_copy(
            ret_out.at[part, me], ret_in.at[part, back], ret_recv.at[part]
        ).start()

    for_sibling(0, 0, 2)
    for_me(0, 0)
    send_corner(0)
    for_me(0, 2)
    send_other(0)
    for_sibling(0, 4)
    for_me(0, 4)
    send_direct(0)
    for_sibling(0, 6)
    for_me(0, 6)
    for_sibling(1, 0, 2, 4, 6)
    send_far(0)
    for_me(1, 0, 2)
    send_corner(1)
    send_partner(0)
    send_other(1)
    for_me(1, 4, 6)
    send_merged(0)
    send_far(1)
    send_direct(1)
    send_partner(1)
    give_back(0)
    send_merged(1)
    give_back(1)

    most = pl.ds(0, owners - 1)
    for copy in gain_copies + sends + list(core_copies.values()) + moved:
        copy.wait_send()
    for part in range(PARTS):
        sent = out_buf.at[part, most]
        pltpu.make_async_copy(sent, sent, disp_send.at[part]).wait()

    take_copy.wait()
    for part in range(PARTS):
        sent = ret_out.at[part, most]
        pltpu.make_async_copy(ret_in.at[part], ret_in.at[part], ret_recv.at[part]).wait()
        pltpu.make_async_copy(sent, sent, ret_send.at[part]).wait()


def add_up(ret_hbm, take_hbm, out_hbm, ret, take_t, out, in_sem, out_sem):
    slots = take_t.shape[1]
    experts_n = slots // CAP
    both = 2 * LANES
    take_copy = pltpu.make_async_copy(take_hbm, take_t, in_sem.at[PARTS])
    copies = [
        pltpu.make_async_copy(ret_hbm.at[part], ret.at[part], in_sem.at[part])
        for part in range(PARTS)
    ]
    take_copy.start()
    for copy in copies:
        copy.start()
    take_copy.wait()
    out_copies = []
    for part in range(PARTS):
        copies[part].wait()
        for p in range(2):
            sides = [
                ret[part, (p * 2 + c) * experts_n : (p * 2 + c + 1) * experts_n].reshape(
                    slots, LANES
                )
                for c in range(2)
            ]
            k = part * 2 + p
            out[k] = dot(take_t[...], jnp.concatenate(sides, axis=1)).astype(BF16)
            start = p * (PARTS * both) + part * both
            copy = pltpu.make_async_copy(
                out.at[k], out_hbm.at[:, pl.ds(start, both)], out_sem.at[k]
            )
            copy.start()
            out_copies.append(copy)
    for copy in out_copies:
        copy.wait()


def per_device(tokens, norm_gain, router, w_gate, w_up, w_down, picked):
    tok_dev, quarter = tokens.shape
    experts_n, capacity = picked.shape
    owners = lax.axis_size("expert")
    hid = w_gate.shape[2]
    width = 4 * quarter
    half = capacity // 2
    slots = experts_n * CAP
    dma = pltpu.SemaphoreType.DMA
    hbm = pl.BlockSpec(memory_space=pl.ANY)
    returned, take_t = pl.pallas_call(
        functools.partial(kernel, owners),
        out_shape=(
            jax.ShapeDtypeStruct((PARTS, owners, CAP, LANES), BF16),
            jax.ShapeDtypeStruct((tok_dev, slots), BF16),
        ),
        in_specs=[hbm] * 7,
        out_specs=(hbm, hbm),
        scratch_shapes=[
            pltpu.VMEM((tok_dev, quarter), BF16),
            pltpu.VMEM((quarter // LANES, LANES), BF16),
            pltpu.VMEM((experts_n, width), BF16),
            pltpu.VMEM((experts_n, capacity), jnp.int32),
            pltpu.VMEM((width, 2 * hid + LANES), BF16),
            pltpu.VMEM((2, hid, width // 2), BF16),
            pltpu.VMEM((4, 16, LANES), BF16),
            pltpu.VMEM((32, LANES), F32),
            pltpu.VMEM((2, experts_n, capacity), F32),
            pltpu.VMEM((slots, LANES), F32),
            pltpu.VMEM((slots, tok_dev), BF16),
            pltpu.VMEM((tok_dev, slots), BF16),
            pltpu.VMEM((capacity, owners * CAP), BF16),
            pltpu.VMEM((owners * CAP, capacity), BF16),
            pltpu.VMEM((PARTS, owners, CAP, LANES), BF16),
            pltpu.VMEM((PARTS, owners, CAP, LANES), BF16),
            pltpu.VMEM((PARTS, 8, 2, capacity, LANES), BF16),
            pltpu.VMEM((capacity, 2 * hid + LANES), F32),
            pltpu.VMEM((capacity, LANES), F32),
            pltpu.VMEM((capacity, hid), BF16),
            pltpu.VMEM((capacity, LANES), F32),
            pltpu.VMEM((PARTS, 8, capacity, LANES), BF16),
            pltpu.VMEM((PARTS, 8, capacity, LANES), BF16),
            pltpu.VMEM((PARTS, 8, capacity, LANES), F32),
            pltpu.VMEM((PARTS, 2, 5, half, LANES), BF16),
            pltpu.VMEM((PARTS, 2, 5, half, LANES), BF16),
            pltpu.VMEM((PARTS, 4, half, LANES), BF16),
            pltpu.VMEM((PARTS, 4, half, LANES), BF16),
            pltpu.VMEM((PARTS, owners, CAP, LANES), BF16),
            dma((4,)),
            dma((1,)),
            dma((3,)),
            dma((3,)),
            dma((4,)),
            dma((PARTS,)),
            dma((PARTS,)),
            dma((60,)),
            dma((64,)),
            dma((16,)),
            dma((16,)),
            dma((20,)),
            dma((20,)),
            dma((8,)),
            dma((8,)),
            dma((PARTS,)),
            dma((PARTS,)),
        ],
        compiler_params=pltpu.CompilerParams(
            collective_id=0, has_side_effects=True, vmem_limit_bytes=56 * 1024 * 1024
        ),
        cost_estimate=pl.CostEstimate(
            flops=2 * capacity * width * 3 * hid,
            bytes_accessed=3 * 2 * width * hid + 4 * tok_dev * quarter,
            transcendentals=capacity * hid,
        ),
    )(
        tokens,
        norm_gain.reshape(quarter // LANES, LANES),
        router.T,
        w_gate,
        w_up,
        w_down,
        picked,
    )
    return pl.pallas_call(
        add_up,
        out_shape=jax.ShapeDtypeStruct((tok_dev, quarter), BF16),
        in_specs=[hbm, hbm],
        out_specs=hbm,
        scratch_shapes=[
            pltpu.VMEM((PARTS, owners, CAP, LANES), BF16),
            pltpu.VMEM((tok_dev, slots), BF16),
            pltpu.VMEM((2 * PARTS, tok_dev, 2 * LANES), BF16),
            dma((PARTS + 1,)),
            dma((2 * PARTS,)),
        ],
        compiler_params=pltpu.CompilerParams(vmem_limit_bytes=56 * 1024 * 1024),
        cost_estimate=pl.CostEstimate(
            flops=2 * tok_dev * slots * quarter,
            bytes_accessed=2 * (2 * slots + tok_dev) * quarter,
            transcendentals=0,
        ),
    )(returned, take_t)


def solution(mesh):
    return jax.shard_map(
        per_device,
        mesh=mesh,
        in_specs=(
            P("expert", "mp"),
            P("mp"),
            P(),
            P("expert", None, "mp"),
            P("expert", None, "mp"),
            P("expert", "mp", None),
            P(),
        ),
        out_specs=P("expert", "mp"),
        check_vma=False,
    )
```

```python
import functools

import jax
import jax.numpy as jnp
from jax import lax
from jax.experimental import pallas as pl
from jax.experimental.pallas import tpu as pltpu
from jax.sharding import PartitionSpec as P

SLICES = 4
CAP = 16
PARTS = 2
LANES = 128
EPS = 1e-06
MESH = pl.DeviceIdType.MESH
F32 = jnp.float32
BF16 = jnp.bfloat16


def remote(src, dst, send, recv, device):
    return pltpu.make_async_remote_copy(
        src_ref=src,
        dst_ref=dst,
        send_sem=send,
        recv_sem=recv,
        device_id=device,
        device_id_type=MESH,
    )


def dot(lhs, rhs):
    return jnp.dot(lhs, rhs, preferred_element_type=F32)


def one_hot(condition):
    return jnp.where(condition, 1.0, 0.0).astype(BF16)


def iota(shape, dim):
    return lax.broadcasted_iota(jnp.int32, shape, dim).astype(F32)


def kernel(
    owners,
    tokens_hbm,
    gain_hbm,
    router_hbm,
    wg_ref,
    wu_ref,
    wd_ref,
    picked_hbm,
    ret_in,
    take_hbm,
    tokens_ref,
    gain_ref,
    router_ref,
    picked_ref,
    w_cat,
    w_down,
    gains,
    gains_f,
    ranked,
    chosen_tok,
    take,
    take_t,
    place,
    place_t,
    out_buf,
    in_buf,
    rows,
    acc,
    squares,
    hidden,
    gate,
    core_out,
    core_in,
    keep,
    y_out,
    y_in,
    x_out,
    x_in,
    ret_out,
    in_sem,
    take_sem,
    w_sem,
    gain_send,
    gain_recv,
    disp_send,
    disp_recv,
    ag_send,
    ag_recv,
    core_send,
    core_recv,
    y_send,
    y_recv,
    x_send,
    x_recv,
    ret_send,
    ret_recv,
):
    tok_dev, quarter = tokens_ref.shape
    experts_n, capacity = picked_ref.shape
    hid = wg_ref.shape[2]
    width = 4 * quarter
    half = capacity // 2
    both = 2 * LANES
    me = lax.axis_index("expert")
    y = lax.axis_index("mp")
    core = lax.rem(me, 2)
    pair = lax.rem(me // 2, 2)
    other = 1 - pair
    my_slice = lax.rem(me, SLICES)
    my_expert = me // SLICES
    sib = (me + 1 - 2 * core, y)
    xpart = (me + 2 - 4 * pair, y)
    y_up = lax.rem(y + 1, 4)
    y_down = lax.rem(y + 3, 4)
    y_far = lax.rem(y + 2, 4)
    up, down = (me, y_up), (me, y_down)

    def peer(r):
        return (lax.rem(me + r, owners), y)

    barrier = pltpu.get_barrier_semaphore()

    def greet(r, carry):
        pl.semaphore_signal(barrier, inc=1, device_id=peer(r), device_id_type=MESH)
        return carry

    for r in range(1, 4):
        pl.semaphore_signal(
            barrier, inc=1, device_id=(me, lax.rem(y + r, 4)), device_id_type=MESH
        )
    lax.fori_loop(1, owners, greet, 0)

    in_copies = [
        pltpu.make_async_copy(src, dst, in_sem.at[k])
        for k, (src, dst) in enumerate(
            [
                (picked_hbm, picked_ref),
                (tokens_hbm, tokens_ref),
                (gain_hbm, gain_ref),
                (router_hbm, router_ref),
            ]
        )
    ]
    w_copies = [
        pltpu.make_async_copy(wg_ref.at[0], w_cat.at[:, pl.ds(0, hid)], w_sem.at[0]),
        pltpu.make_async_copy(wu_ref.at[0], w_cat.at[:, pl.ds(hid, hid)], w_sem.at[1]),
    ]
    for copy in in_copies + w_copies:
        copy.start()

    tri = one_hot(iota((capacity, capacity), 0) <= iota((capacity, capacity), 1))
    in_copies[0].wait()
    rel = picked_ref[...] - me * tok_dev
    mine = jnp.where((rel >= 0) & (rel < tok_dev), 1.0, 0.0)
    ranked[0] = dot(mine.astype(BF16), tri) * mine
    ranked[1] = rel.astype(F32) + 1.0
    slot_no = iota((CAP, capacity), 0) + 1.0
    lane_no = iota((CAP, tok_dev), 1)
    for e in range(experts_n):
        hit = ranked[0, e : e + 1, :] == slot_no
        found = jnp.where(hit, ranked[1, e : e + 1, :], 0.0)
        token = jnp.sum(found, axis=1, keepdims=True) - 1.0
        take[e * CAP : (e + 1) * CAP, :] = one_hot(token == lane_no)
        chosen_tok[e * CAP : (e + 1) * CAP, :] = jnp.broadcast_to(token, (CAP, LANES))

    row = picked_ref[pl.ds(my_expert, 1), :]
    low = lax.broadcasted_iota(jnp.int32, (owners, capacity), 0) * tok_dev
    held = jnp.where((row >= low) & (row < low + tok_dev), 1.0, 0.0)
    slot_at = dot(held.astype(BF16), tri) - 1.0 + iota((owners, capacity), 0) * CAP
    flat = jnp.sum(held * slot_at, axis=0, keepdims=True)
    flat_col = jnp.broadcast_to(flat, (LANES, capacity)).T
    down_no = iota((LANES, capacity), 0)
    across_no = iota((capacity, LANES), 1)
    for j in range(owners * CAP // LANES):
        span = slice(j * LANES, (j + 1) * LANES)
        place_t[span, :] = one_hot(flat == down_no + j * LANES)
        place[:, span] = one_hot(flat_col == across_no + j * LANES)
    take_t[...] = one_hot(chosen_tok[...].T[0:1, :] == iota((tok_dev, experts_n * CAP), 0))
    take_copy = pltpu.make_async_copy(take_t, take_hbm, take_sem.at[0])
    take_copy.start()

    def gather(part):
        for p in range(2):
            start = p * quarter // 2 + part * both
            found = dot(take[...], tokens_ref[:, start : start + both]).astype(BF16)
            for e in range(experts_n):
                for c in range(2):
                    out_buf[part, e * SLICES + p * 2 + c] = found[
                        e * CAP : (e + 1) * CAP, c * LANES : (c + 1) * LANES
                    ]

    in_copies[1].wait()
    gather(0)
    gather(1)
    in_copies[2].wait()
    in_copies[3].wait()
    select = one_hot(iota((experts_n, LANES), 0) == my_expert.astype(F32))
    for j in range(8):
        span = slice(j * width // 8, (j + 1) * width // 8)
        w_cat[span, 2 * hid :] = lax.dot_general(
            router_ref[:, span],
            select,
            (((0,), (0,)), ((), ())),
            preferred_element_type=F32,
        ).astype(BF16)
    gains[y] = jnp.concatenate([gain_ref[...], gain_ref[...]], axis=0)

    pl.semaphore_wait(barrier, owners - 1 + 3)

    targets = [
        (y_far, other),
        (y_up, other),
        (y_down, other),
        (y_far, pair),
        (y_up, pair),
        (y_down, pair),
        (y, other),
        (y, pair),
    ]

    def load_down():
        for part in range(PARTS):
            for k, (at_y, at_pair) in enumerate(targets):
                for side, c in enumerate((core, 1 - core)):
                    start = at_y * quarter + at_pair * (quarter // 2) + part * both + c * LANES
                    pltpu.make_async_copy(
                        wd_ref.at[0, :, pl.ds(pl.multiple_of(start, LANES), LANES)],
                        w_down.at[side, :, pl.ds((part * 8 + k) * LANES, LANES)],
                        w_sem.at[2],
                    ).start()

    def dispatch(part):
        for side in range(2):

            def start(j, carry):
                d = 2 * lax.rem(me // 2 + j, owners // 2) + side
                remote(
                    out_buf.at[part, d],
                    in_buf.at[part, me],
                    disp_send.at[part],
                    disp_recv.at[part],
                    (d, y),
                ).start()
                return carry

            first = 1 - core if side == 0 else core
            lax.fori_loop(first, owners // 2, start, 0)
        pltpu.make_async_copy(
            out_buf.at[part, me], in_buf.at[part, me], disp_recv.at[part]
        ).start()

    gain_copies = []
    for r in range(1, 4):
        copy = remote(
            gains.at[y],
            gains.at[y],
            gain_send.at[r - 1],
            gain_recv.at[y],
            (me, lax.rem(y + r, 4)),
        )
        copy.start()
        gain_copies.append(copy)
    dispatch(0)
    dispatch(1)
    load_down()

    for r in range(1, 4):
        at = lax.rem(y + r, 4)
        remote(gains.at[at], gains.at[at], gain_send.at[0], gain_recv.at[at], up).wait_recv()
    for at in range(4):
        gains_f[at * 8 : (at + 1) * 8, :] = gains[at][:8, :].astype(F32)
    w_copies[0].wait()
    w_copies[1].wait()

    def scale(q, carry):
        start = pl.multiple_of(q * LANES, LANES)
        column = jnp.broadcast_to(gains_f[pl.ds(q, 1), :], (LANES, LANES)).T
        for j in range(2 * hid // LANES + 1):
            cols = slice(j * LANES, (j + 1) * LANES)
            w_cat[pl.ds(start, LANES), cols] = (
                w_cat[pl.ds(start, LANES), cols].astype(F32) * column
            ).astype(BF16)
        return carry

    lax.fori_loop(0, width // LANES, scale, 0, unroll=4)

    def block(at_y, at_pair):
        return at_y * 2 + at_pair

    def ag(part, b, c, h, k, device):
        at = rows.at[part, b, c, pl.ds(h * half, half)]
        number = ((part * 8 + b) * 2 + c) * 2 + h
        return remote(at, at, ag_send.at[k], ag_recv.at[number], device)

    sends = []

    def go(part, b, h, *devices):
        for device in devices:
            copy = ag(part, b, core, h, len(sends), device)
            copy.start()
            sends.append(copy)

    def pass_on(part, b, h, *devices):
        ag(part, b, core, h, 0, sib).wait_recv()
        go(part, b, h, *devices, sib)

    def begin(part):
        pltpu.make_async_copy(in_buf.at[part], in_buf.at[part], disp_recv.at[part]).wait()
        b = block(y, pair)
        arrived = in_buf[part].reshape(owners * CAP, LANES)
        for h in range(2):
            span = slice(h * half, (h + 1) * half)
            rows[part, b, core, span] = dot(place[span, :], arrived).astype(BF16)
            if h == 1:
                go(part, b, 1, down)
            go(part, b, h, xpart, up, sib)
        go(part, b, 0, down)

    def from_neighbours(part):
        pass_on(part, block(y_down, pair), 0, up)
        pass_on(part, block(y_up, pair), 1, down)

    def rest_of_neighbours(part):
        pass_on(part, block(y_down, pair), 1)
        pass_on(part, block(y_up, pair), 0)

    def from_partner(part, h):
        pass_on(part, block(y, other), h, up, down)

    def from_far(part):
        for h in range(2):
            pass_on(part, block(y_far, pair), h, xpart)

    def from_corners(part):
        for h in range(2):
            pass_on(part, block(y_down, other), h)
            pass_on(part, block(y_up, other), h)

    def from_far_corner(part):
        for h in range(2):
            pass_on(part, block(y_far, other), h)

    def product(part, at_y, at_pair, first=False):
        b = block(at_y, at_pair)
        for h in range(2):
            ag(part, b, 1 - core, h, 0, sib).wait_recv()
        start = pl.multiple_of(
            at_y * quarter + at_pair * (quarter // 2) + part * both, both
        )
        left, right = rows[part, b, 0], rows[part, b, 1]
        new = dot(jnp.concatenate([left, right], axis=1), w_cat[pl.ds(start, both), :])
        left, right = left.astype(F32), right.astype(F32)
        square = left * left + right * right
        if first:
            acc[...] = new
            squares[...] = square
        else:
            acc[...] += new
            squares[...] += square

    begin(0)
    from_neighbours(0)
    from_partner(0, 0)
    begin(1)
    from_neighbours(1)
    from_partner(0, 1)
    from_partner(1, 0)
    rest_of_neighbours(0)
    from_far(0)
    from_partner(1, 1)
    product(0, y, pair, first=True)
    product(0, y_down, pair)
    product(0, y_up, pair)
    rest_of_neighbours(1)
    from_far(1)
    product(0, y, other)
    product(1, y, pair)
    product(0, y_far, pair)
    from_corners(0)
    product(1, y_down, pair)
    product(1, y_up, pair)
    product(1, y, other)
    from_far_corner(0)
    product(0, y_down, other)
    product(0, y_up, other)
    product(0, y_far, other)
    from_corners(1)
    product(1, y_far, pair)
    product(1, y_down, other)
    product(1, y_up, other)
    from_far_corner(1)
    product(1, y_far, other)

    total = jnp.sum(squares[...], axis=1, keepdims=True)
    inv = lax.rsqrt(total * (1.0 / width) + EPS)
    hidden[...] = (
        jax.nn.gelu(acc[:, :hid] * inv, approximate=True) * (acc[:, hid : 2 * hid] * inv)
    ).astype(BF16)
    gate[...] = jax.nn.sigmoid(acc[:, 2 * hid :] * inv).astype(BF16).astype(F32)
    pltpu.make_async_copy(w_down, w_down, w_sem.at[2]).wait()

    top, bottom = slice(0, half), slice(half, capacity)
    core_copies = {}

    def partial(part, k, side):
        start = (part * 8 + k) * LANES
        return dot(hidden[...], w_down[side, :, start : start + both])

    def for_sibling(part, *firsts):
        for first in firsts:
            value = partial(part, first, 1)
            for k in (first, first + 1):
                at = (k - first) * LANES
                core_out[part, k] = value[:, at : at + LANES].astype(BF16)
                number = part * 8 + k
                copy = remote(
                    core_out.at[part, k],
                    core_in.at[part, k],
                    core_send.at[number],
                    core_recv.at[number],
                    sib,
                )
                copy.start()
                core_copies[part, k] = copy

    def for_me(part, *firsts):
        for first in firsts:
            value = partial(part, first, 0)
            keep[part, first] = value[:, :LANES]
            keep[part, first + 1] = value[:, LANES:]

    def chip(part, k):
        core_copies[part, k].wait_recv()
        return keep[part, k] + core_in[part, k].astype(F32)

    moved = []

    def y_copy(part, way, m):
        number = (part * 2 + way) * 5 + m
        return remote(
            y_out.at[part, way, m],
            y_in.at[part, way, m],
            y_send.at[number],
            y_recv.at[number],
            (up, down)[way],
        )

    def y_go(part, way, m, value):
        y_out[part, way, m] = value.astype(BF16)
        copy = y_copy(part, way, m)
        copy.start()
        moved.append(copy)

    def y_got(part, way, m):
        y_copy(part, way, m).wait_recv()
        return y_in[part, way, m].astype(F32)

    def x_copy(part, m):
        number = part * 4 + m
        return remote(
            x_out.at[part, m], x_in.at[part, m], x_send.at[number], x_recv.at[number], xpart
        )

    def x_go(part, m, value):
        x_out[part, m] = value.astype(BF16)
        copy = x_copy(part, m)
        copy.start()
        moved.append(copy)

    def x_got(part, m):
        x_copy(part, m).wait_recv()
        return x_in[part, m].astype(F32)

    def send_corner(part):
        value = chip(part, 0)
        x_go(part, 0, value[top])
        x_go(part, 1, value[bottom])

    def send_other(part):
        for way in range(2):
            value = chip(part, 1 + way)
            y_go(part, way, 0, value[top])
            y_go(part, way, 1, value[bottom])

    def send_direct(part):
        value = chip(part, 4)
        y_go(part, 0, 2, value[top])
        keep[part, 4, bottom] = value[bottom]
        value = chip(part, 5)
        y_go(part, 1, 2, value[bottom])
        keep[part, 5, top] = value[top]

    def send_far(part):
        value = chip(part, 3)
        y_go(part, 1, 3, value[top] + x_got(part, 0))
        y_go(part, 0, 3, value[bottom] + x_got(part, 1))

    def send_merged(part):
        y_go(part, 1, 4, keep[part, 5, top] + y_got(part, 1, 3))
        y_go(part, 0, 4, keep[part, 4, bottom] + y_got(part, 0, 3))

    def send_partner(part):
        value = chip(part, 6)
        x_go(part, 2, value[top] + y_got(part, 0, 0) + y_got(part, 1, 0))
        x_go(part, 3, value[bottom] + y_got(part, 0, 1) + y_got(part, 1, 1))

    back = my_slice * experts_n + my_expert

    def give_back(part):
        value = chip(part, 7)
        upper = value[top] + y_got(part, 0, 2) + y_got(part, 1, 4) + x_got(part, 2)
        lower = value[bottom] + y_got(part, 1, 2) + y_got(part, 0, 4) + x_got(part, 3)
        gated = (jnp.concatenate([upper, lower], axis=0) * gate[...]).astype(BF16)
        ret_out[part] = dot(place_t[...], gated).astype(BF16).reshape(owners, CAP, LANES)

        def start(r, carry):
            d, _ = peer(r)
            remote(
                ret_out.at[part, d],
                ret_in.at[part, back],
                ret_send.at[part],
                ret_recv.at[part],
                (d, y),
            ).start()
            return carry

        lax.fori_loop(1, owners, start, 0)
        pltpu.make_async_copy(
            ret_out.at[part, me], ret_in.at[part, back], ret_recv.at[part]
        ).start()

    for_sibling(0, 0, 2)
    for_me(0, 0)
    send_corner(0)
    for_me(0, 2)
    send_other(0)
    for_sibling(0, 4)
    for_me(0, 4)
    send_direct(0)
    for_sibling(0, 6)
    for_me(0, 6)
    for_sibling(1, 0, 2, 4, 6)
    send_far(0)
    for_me(1, 0, 2)
    send_corner(1)
    send_partner(0)
    send_other(1)
    for_me(1, 4, 6)
    send_merged(0)
    send_far(1)
    send_direct(1)
    send_partner(1)
    give_back(0)
    send_merged(1)
    give_back(1)

    most = pl.ds(0, owners - 1)
    for copy in gain_copies + sends + list(core_copies.values()) + moved:
        copy.wait_send()
    for part in range(PARTS):
        sent = out_buf.at[part, most]
        pltpu.make_async_copy(sent, sent, disp_send.at[part]).wait()

    take_copy.wait()
    for part in range(PARTS):
        sent = ret_out.at[part, most]
        pltpu.make_async_copy(ret_in.at[part], ret_in.at[part], ret_recv.at[part]).wait()
        pltpu.make_async_copy(sent, sent, ret_send.at[part]).wait()


def add_up(ret_hbm, take_hbm, out_hbm, ret, take_t, out, in_sem, out_sem):
    slots = take_t.shape[1]
    experts_n = slots // CAP
    both = 2 * LANES
    take_copy = pltpu.make_async_copy(take_hbm, take_t, in_sem.at[PARTS])
    copies = [
        pltpu.make_async_copy(ret_hbm.at[part], ret.at[part], in_sem.at[part])
        for part in range(PARTS)
    ]
    take_copy.start()
    for copy in copies:
        copy.start()
    take_copy.wait()
    out_copies = []
    for part in range(PARTS):
        copies[part].wait()
        for p in range(2):
            sides = [
                ret[part, (p * 2 + c) * experts_n : (p * 2 + c + 1) * experts_n].reshape(
                    slots, LANES
                )
                for c in range(2)
            ]
            k = part * 2 + p
            out[k] = dot(take_t[...], jnp.concatenate(sides, axis=1)).astype(BF16)
            start = p * (PARTS * both) + part * both
            copy = pltpu.make_async_copy(
                out.at[k], out_hbm.at[:, pl.ds(start, both)], out_sem.at[k]
            )
            copy.start()
            out_copies.append(copy)
    for copy in out_copies:
        copy.wait()


def per_device(tokens, norm_gain, router, w_gate, w_up, w_down, picked):
    tok_dev, quarter = tokens.shape
    experts_n, capacity = picked.shape
    owners = lax.axis_size("expert")
    hid = w_gate.shape[2]
    width = 4 * quarter
    half = capacity // 2
    slots = experts_n * CAP
    dma = pltpu.SemaphoreType.DMA
    hbm = pl.BlockSpec(memory_space=pl.ANY)
    returned, take_t = pl.pallas_call(
        functools.partial(kernel, owners),
        out_shape=(
            jax.ShapeDtypeStruct((PARTS, owners, CAP, LANES), BF16),
            jax.ShapeDtypeStruct((tok_dev, slots), BF16),
        ),
        in_specs=[hbm] * 7,
        out_specs=(hbm, hbm),
        scratch_shapes=[
            pltpu.VMEM((tok_dev, quarter), BF16),
            pltpu.VMEM((quarter // LANES, LANES), BF16),
            pltpu.VMEM((experts_n, width), BF16),
            pltpu.VMEM((experts_n, capacity), jnp.int32),
            pltpu.VMEM((width, 2 * hid + LANES), BF16),
            pltpu.VMEM((2, hid, width // 2), BF16),
            pltpu.VMEM((4, 16, LANES), BF16),
            pltpu.VMEM((32, LANES), F32),
            pltpu.VMEM((2, experts_n, capacity), F32),
            pltpu.VMEM((slots, LANES), F32),
            pltpu.VMEM((slots, tok_dev), BF16),
            pltpu.VMEM((tok_dev, slots), BF16),
            pltpu.VMEM((capacity, owners * CAP), BF16),
            pltpu.VMEM((owners * CAP, capacity), BF16),
            pltpu.VMEM((PARTS, owners, CAP, LANES), BF16),
            pltpu.VMEM((PARTS, owners, CAP, LANES), BF16),
            pltpu.VMEM((PARTS, 8, 2, capacity, LANES), BF16),
            pltpu.VMEM((capacity, 2 * hid + LANES), F32),
            pltpu.VMEM((capacity, LANES), F32),
            pltpu.VMEM((capacity, hid), BF16),
            pltpu.VMEM((capacity, LANES), F32),
            pltpu.VMEM((PARTS, 8, capacity, LANES), BF16),
            pltpu.VMEM((PARTS, 8, capacity, LANES), BF16),
            pltpu.VMEM((PARTS, 8, capacity, LANES), F32),
            pltpu.VMEM((PARTS, 2, 5, half, LANES), BF16),
            pltpu.VMEM((PARTS, 2, 5, half, LANES), BF16),
            pltpu.VMEM((PARTS, 4, half, LANES), BF16),
            pltpu.VMEM((PARTS, 4, half, LANES), BF16),
            pltpu.VMEM((PARTS, owners, CAP, LANES), BF16),
            dma((4,)),
            dma((1,)),
            dma((3,)),
            dma((3,)),
            dma((4,)),
            dma((PARTS,)),
            dma((PARTS,)),
            dma((60,)),
            dma((64,)),
            dma((16,)),
            dma((16,)),
            dma((20,)),
            dma((20,)),
            dma((8,)),
            dma((8,)),
            dma((PARTS,)),
            dma((PARTS,)),
        ],
        compiler_params=pltpu.CompilerParams(
            collective_id=0, has_side_effects=True, vmem_limit_bytes=56 * 1024 * 1024
        ),
        cost_estimate=pl.CostEstimate(
            flops=2 * capacity * width * 3 * hid,
            bytes_accessed=3 * 2 * width * hid + 4 * tok_dev * quarter,
            transcendentals=capacity * hid,
        ),
    )(
        tokens,
        norm_gain.reshape(quarter // LANES, LANES),
        router.T,
        w_gate,
        w_up,
        w_down,
        picked,
    )
    return pl.pallas_call(
        add_up,
        out_shape=jax.ShapeDtypeStruct((tok_dev, quarter), BF16),
        in_specs=[hbm, hbm],
        out_specs=hbm,
        scratch_shapes=[
            pltpu.VMEM((PARTS, owners, CAP, LANES), BF16),
            pltpu.VMEM((tok_dev, slots), BF16),
            pltpu.VMEM((2 * PARTS, tok_dev, 2 * LANES), BF16),
            dma((PARTS + 1,)),
            dma((2 * PARTS,)),
        ],
        compiler_params=pltpu.CompilerParams(vmem_limit_bytes=56 * 1024 * 1024),
        cost_estimate=pl.CostEstimate(
            flops=2 * tok_dev * slots * quarter,
            bytes_accessed=2 * (2 * slots + tok_dev) * quarter,
            transcendentals=0,
        ),
    )(returned, take_t)


def solution(mesh):
    return jax.shard_map(
        per_device,
        mesh=mesh,
        in_specs=(
            P("expert", "mp"),
            P("mp"),
            P(),
            P("expert", None, "mp"),
            P("expert", None, "mp"),
            P("expert", "mp", None),
            P(),
        ),
        out_specs=P("expert", "mp"),
        check_vma=False,
    )
```
